128 devices in a mesh: corr: 16 (over y, x), lc: 8 (over z, core).
Axes of the slice: x: 4, y: 4, z: 4, core: 2. Of those that a mesh axis runs over, the one named last changes fastest.
Arguments:
- density: float32 [4, 3, 2048, 1024], P(None, None, 'corr', 'lc'), may hold values from 0.002 to 0.16
- cap_code: int32 [4, 2048, 1024], P(None, 'corr', 'lc'), may hold values from 0 to 7
- jam_code: int32 [4, 2048, 1024], P(None, 'corr', 'lc'), may hold values from 0 to 3
- adjacency: int32 [3, 2048, 1024], P(None, 'corr', 'lc'), may hold values 0 or 1
- ramp_code: int32 [8, 4, 1024], P(None, None, 'lc'), may hold values from 0 to 7
- feed_a: int32 [1024], P('lc'), may hold values from 0 to 1023, each once
- feed_b: int32 [1024], P('lc'), may hold values from 0 to 1023, each once
- turn_share: float32 [1024], P('lc'), may hold values from 0.2 to 0.8
- priority: float32 [1024], P('lc'), may hold values from 0.2 to 0.8
- cap_table: float32 [8], replicated, may hold values from 0.1 to 0.25
- jam_table: float32 [4], replicated, may hold values from 0.8 to 1.2
- change_coef: float32 [3], replicated, may hold values from 0.05 to 0.2
Outputs:
- traffic: float32 [4, 3, 2048, 1024], P(None, None, 'corr', 'lc')
- queue_count: float32 [2048, 1024], P('corr', 'lc')
The draws below stay inside these ranges and needn't reach their ends.
Inputs may be any that keep to these rules, and one draw needn't show every extreme that they name: `feed_a`: every corridor appears exactly once. `feed_b`: every corridor appears exactly once.
All inputs are finite; a program needn't handle non-finite values. No bound on the sum of `adjacency` on one device may be relied on, other than what follows from the above.
Results may differ from the reference program's by a relative error of at most 0.0001.
Values sent between devices are 32-bit elements; how exact they have to be, the bound alone decides.
No kernel may reach another device: no remote copies, remote signals or barrier semaphores. Data moves between devices by JAX's collectives and lax.ppermute only.
A program may use at most 64 MiB of HBM per device.

```python
import math
import jax
import jax.numpy as jnp
from jax import lax

LANES = 4
CLASSES = 3
STEPS = 8
CELLS = 2048
CORRIDORS = 1024


def with_ends(values, stream_key, least, largest):
    index_at = [jax.random.randint(jax.random.fold_in(stream_key, axis), (), 0, length) for axis, length in enumerate(values.shape)]
    widest = values.shape.index(max(values.shape))
    next_to = index_at[:widest] + [(index_at[widest] + 1) % values.shape[widest]] + index_at[widest + 1:]
    return values.at[tuple(index_at)].set(least).at[tuple(next_to)].set(largest)


def block_levels(key, extent, pieces, low, high):
    def one(dim, blocks):
        heights = jax.random.uniform(jax.random.fold_in(jax.random.fold_in(key, 6), dim), (blocks,), jnp.float32, low / len(pieces), high / len(pieces))
        return jnp.repeat(jnp.exp(heights), extent[dim] // blocks).reshape((-1,) + (1,) * (len(extent) - dim - 1))

    level = one(*pieces[0])
    for cut in pieces[1:]:
        level = level * one(*cut)
    return level


def setup_inputs(seed: int = 0) -> dict:
    keys = jax.random.split(jax.random.key(seed), 13)
    density = jnp.clip(0.002 + 0.157999996 * jax.random.uniform(keys[0], (LANES, CLASSES, CELLS, CORRIDORS), jnp.float32) ** block_levels(keys[0], (LANES, CLASSES, CELLS, CORRIDORS), ((2, 16), (3, 8)), -0.2, 0.2), 0.002, 0.16)
    cap_code = with_ends(jax.random.randint(keys[1], (LANES, CELLS, CORRIDORS), 0, 8), jax.random.fold_in(keys[1], 1), 0, 7).astype(jnp.int32)
    jam_code = with_ends(jax.random.randint(keys[2], (LANES, CELLS, CORRIDORS), 0, 4), jax.random.fold_in(keys[2], 1), 0, 3).astype(jnp.int32)
    adjacency = with_ends((jax.random.randint(keys[3], (LANES - 1, CELLS, CORRIDORS), 0, 4) < 3).astype(jnp.int32), jax.random.fold_in(keys[3], 1), 0, 1)
    ramp_code = with_ends(jax.random.randint(keys[4], (STEPS, LANES, CORRIDORS), 0, 8), jax.random.fold_in(keys[4], 1), 0, 7).astype(jnp.int32)
    feed_a = jax.random.permutation(keys[5], CORRIDORS).astype(jnp.int32)
    feed_b = jax.random.permutation(keys[6], CORRIDORS).astype(jnp.int32)
    turn_share = jnp.clip(0.2 + 0.6 * jax.random.uniform(keys[7], (CORRIDORS,), jnp.float32) ** block_levels(keys[7], (CORRIDORS,), ((0, 8),), -0.2, 0.2), 0.2, 0.8)
    priority = jnp.clip(0.2 + 0.6 * jax.random.uniform(keys[8], (CORRIDORS,), jnp.float32) ** block_levels(keys[8], (CORRIDORS,), ((0, 8),), -0.2, 0.2), 0.2, 0.8)
    cap_table = jnp.clip(jnp.exp(jax.random.uniform(keys[9], (8,), jnp.float32, math.log(0.1), math.log(0.25))), 0.1, 0.25)
    jam_table = jnp.clip(jax.random.uniform(keys[10], (4,), jnp.float32, 0.8, 1.2), 0.8, 1.2)
    change_coef = jnp.clip(jnp.exp(jax.random.uniform(keys[11], (CLASSES,), jnp.float32, math.log(0.05), math.log(0.2))), 0.05, 0.2)
    return {"density": density, "cap_code": cap_code, "jam_code": jam_code, "adjacency": adjacency, "ramp_code": ramp_code, "feed_a": feed_a, "feed_b": feed_b, "turn_share": turn_share, "priority": priority, "cap_table": cap_table, "jam_table": jam_table, "change_coef": change_coef}


pce_weights = (1.0, 1.5, 2.5)
ramp_unit = 0.01
ramp_fraction = (0.56, 0.16, 0.08)


def lookup(codes, values):
    looked = jnp.zeros(codes.shape, values.dtype)
    for code_value in range(values.shape[0]):
        looked = looked + jnp.where(codes == code_value, values[code_value], 0.0)
    return looked


def pce_total(state):
    totals = state[:, 0] * pce_weights[0]
    for class_index in range(1, len(pce_weights)):
        totals = totals + state[:, class_index] * pce_weights[class_index]
    return totals


def cell_terms(state, totals, capacity, jam_cap, wave_speed):
    speeds = capacity / jnp.maximum(totals, 2.0 * capacity)
    demand = state * speeds[:, None]
    pce_demand = totals * speeds
    supply = jnp.maximum(jnp.minimum(capacity, wave_speed * (jam_cap - totals)), 0.0)
    return demand, pce_demand, supply


def middle(first_term, second_term, third_term):
    return jnp.maximum(jnp.minimum(first_term, second_term), jnp.minimum(jnp.maximum(first_term, second_term), third_term))


def junction(take_a, take_b, supply, share_a, share_b):
    class_count = take_a.shape[1] - 1
    need_a = take_a[:, class_count]
    need_b = take_b[:, class_count]
    pass_a = jnp.minimum(need_a, middle(need_a, supply - need_b, share_a))
    pass_b = jnp.minimum(need_b, middle(need_b, supply - need_a, share_b))
    rate_a = pass_a / need_a
    rate_b = pass_b / need_b
    inflow = take_a[:, :class_count] * rate_a[:, None] + take_b[:, :class_count] * rate_b[:, None]
    spare = jnp.maximum((supply - pass_a) - pass_b, 0.0)
    return inflow, spare, rate_a, rate_b


def ramp_inflow(ramp_row, spare):
    ramp_flow = jnp.minimum(ramp_row.astype(jnp.float32) * ramp_unit, spare)
    fractions = jnp.array(ramp_fraction, dtype=jnp.float32)
    return ramp_flow[:, None] * fractions[None, :, None]


def lane_change(state, change_rate):
    moving = change_rate * (state[:-1] - state[1:])
    zeros_row = jnp.zeros_like(state[:1])
    return (state - jnp.concatenate([moving, zeros_row], 0)) + jnp.concatenate([zeros_row, moving], 0)


def reference(density, cap_code, jam_code, adjacency, ramp_code, feed_a, feed_b, turn_share, priority, cap_table, jam_table, change_coef):
    capacity = lookup(cap_code, cap_table)
    jam_cap = lookup(jam_code, jam_table)
    critical = 2.0 * capacity
    wave_speed = capacity / (jam_cap - critical)
    change_rate = change_coef[None, :, None, None] * adjacency.astype(jnp.float32)[:, None]
    class_count = density.shape[1]
    state = density
    totals = pce_total(state)
    accumulated = jnp.zeros(capacity.shape[1:], jnp.float32)
    for step_index in range(STEPS):
        demand, pce_demand, supply = cell_terms(state, totals, capacity, jam_cap, wave_speed)
        ratios = jnp.minimum(pce_demand[:, :-1], supply[:, 1:]) / pce_demand[:, :-1]
        inner = demand[:, :, :-1] * ratios[:, None]
        end_vals = jnp.concatenate([demand[:, :, -1], pce_demand[:, None, -1]], 1)
        part_a = turn_share * end_vals
        part_b = (1.0 - turn_share) * end_vals
        take_a = jnp.take(part_a, feed_a, axis=2)
        take_b = jnp.take(part_b, feed_b, axis=2)
        head_supply = supply[:, 0]
        inflow, spare, rate_a, rate_b = junction(take_a, take_b, head_supply, priority * head_supply, (1.0 - priority) * head_supply)
        arriving = inflow + ramp_inflow(ramp_code[step_index], spare)
        back_a = jnp.zeros_like(rate_a).at[:, feed_a].set(rate_a)
        back_b = jnp.zeros_like(rate_b).at[:, feed_b].set(rate_b)
        leaving = part_a[:, :class_count] * back_a[:, None] + part_b[:, :class_count] * back_b[:, None]
        in_flux = jnp.concatenate([arriving[:, :, None], inner], 2)
        out_flux = jnp.concatenate([inner, leaving[:, :, None]], 2)
        state = (state + in_flux) - out_flux
        state = lane_change(state, change_rate)
        totals = pce_total(state)
        excess = jnp.sum(totals - critical, 0) * 0.25
        running = jnp.cumsum(excess, 0)
        lowest = jnp.minimum(lax.cummin(running, axis=0), 0.0)
        accumulated = accumulated + (running - lowest)
    return state, accumulated / float(STEPS * CELLS)
```

```python
import jax
import jax.numpy as jnp
from jax import lax
from jax.experimental import pallas as pl
from jax.experimental.pallas import tpu as pltpu
from jax.sharding import PartitionSpec as P

STEPS = 8
LANES = 4
CLASSES = 3
ROWS = 16
WIDTH = 128
CELLS_HERE = 128
BIG = 1e30
F32 = jnp.float32
RAMP_UNIT = 0.01
RAMP_FRACTION = (0.56, 0.16, 0.08)
VMEM_BYTES = 40 * 1024 * 1024

HEAD_DEPTH = 27
TAIL_DEPTH = 35
RAMP_ROW = 108
FEED_ROW = 140
SHARE_ROW = 141
INVERSE_ROW = 142
RECORD = 152


def inverse(x):
    r = pl.reciprocal(x, approx=True)
    return r * (2.0 - x * r)


def total_of(state):
    return state[0] + 1.5 * state[1] + 2.5 * state[2]


def supply_of(totals, cap, jam, wave):
    return jnp.maximum(jnp.minimum(cap, wave * (jam - totals)), 0.0)


def sent_share(totals, cap, next_supply):
    return jnp.minimum(0.5, jnp.minimum(cap, next_supply) * inverse(totals))


def pick(code, table, count):
    values = [table[i] for i in range(count)]
    bit = 1
    while len(values) > 1:
        on = (code & bit) != 0
        values = [jnp.where(on, values[i + 1], values[i]) for i in range(0, len(values), 2)]
        bit *= 2
    return values[0]


def wave_of(cap, jam):
    return cap / (jam - 2.0 * cap)


def lane_change(state, adjacent, coef):
    moving = [
        [(adjacent[p] * coef[k]) * (state[p][k] - state[p + 1][k]) for k in range(CLASSES)]
        for p in range(LANES - 1)
    ]
    out = []
    for lane in range(LANES):
        row = []
        for k in range(CLASSES):
            value = state[lane][k]
            if lane < LANES - 1:
                value = value - moving[lane][k]
            if lane > 0:
                value = value + moving[lane - 1][k]
            row.append(value)
        out.append(row)
    return out


def middle(a, b, c):
    return jnp.maximum(jnp.minimum(a, b), jnp.minimum(jnp.maximum(a, b), c))


def window(count, refs, step, coef, inject, mask, scan):
    st, tot, cap, jam, wave, adj, level, acc, low = refs
    last = count - 1

    def supply(v):
        return [
            supply_of(tot[lane, v], cap[lane, v], jam[lane, v], wave[lane, v])
            for lane in range(LANES)
        ]

    def flux(v, next_supply):
        out = []
        for lane in range(LANES):
            share = sent_share(tot[lane, v], cap[lane, v], next_supply[lane])
            out.append([st[lane * CLASSES + k, v] * share for k in range(CLASSES)])
        return out

    wrapped = [pltpu.roll(x, 7, 0) for x in supply(0)]
    final = flux(last, wrapped)
    before = [[pltpu.roll(x, 1, 0) for x in row] for row in final]
    running = lowest = None
    for v in range(count):
        leaving = flux(v, supply(v + 1)) if v < last else final
        came, gone = inject(v, before, leaving)
        state = [
            [(st[lane * CLASSES + k, v] + came[lane][k]) - gone[lane][k] for k in range(CLASSES)]
            for lane in range(LANES)
        ]
        state = lane_change(state, [adj[p, v] for p in range(LANES - 1)], coef)
        sums = []
        for lane in range(LANES):
            for k in range(CLASSES):
                st[lane * CLASSES + k, v] = state[lane][k]
            sums.append(total_of(state[lane]))
            tot[lane, v] = sums[lane]
        excess = 0.25 * ((sums[0] + sums[1]) + (sums[2] + sums[3])) - level[v]
        excess = jnp.where(mask(v), excess, 0.0)
        running = excess if running is None else running + excess
        lowest = running if lowest is None else jnp.minimum(lowest, running)
        acc[1, v] = running
        low[step, v] = lowest
        before = leaving
    carry, floor = scan(running, lowest)
    for v in range(count):
        acc[0, v] = acc[0, v] + (carry + acc[1, v])
        low[step, v] = jnp.minimum(floor, carry + low[step, v])


def fill(count, stride, refs, density, cap_code, jam_code, adjacency, cap_table, jam_table):
    st, tot, cap, jam, wave, adj, level, acc = refs
    for v in range(count):
        rows = pl.ds(v, 8, stride=stride)
        around = None
        for lane in range(LANES):
            state = [density(lane * CLASSES + k, rows) for k in range(CLASSES)]
            for k in range(CLASSES):
                st[lane * CLASSES + k, v] = state[k]
            tot[lane, v] = total_of(state)
            c = pick(cap_code(lane, rows), cap_table, 8)
            j = pick(jam_code(lane, rows), jam_table, 4)
            cap[lane, v] = c
            jam[lane, v] = j
            wave[lane, v] = wave_of(c, j)
            around = c if around is None else around + c
        for p in range(LANES - 1):
            adj[p, v] = adjacency(p, rows)
        level[v] = 0.5 * around
        acc[0, v] = jnp.zeros((8, WIDTH), F32)


def pack_kernel(
    cap_table, jam_table, coef_ref, feed_a, feed_b, feed_a_row, feed_b_row, share_row, prio_row,
    ramp, d_lo, d_hi, c_lo, c_hi, j_lo, j_hi, a_lo, a_hi, fwd, bwd, zone,
):
    tail = lax.axis_index("corr") == ROWS - 1
    place = lax.axis_index("lc")
    for out, d, c, j, a in ((bwd, d_lo, c_lo, j_lo, a_lo), (fwd, d_hi, c_hi, j_hi, a_hi)):
        row = 0
        for ref, n in ((d, 12), (c, 4), (j, 4), (a, 3)):
            for i in range(n):
                out[pl.ds(row * 8, 8), :] = ref[i].astype(F32)
                row += 1
    coef = [coef_ref[k] for k in range(CLASSES)]

    def own(lo, hi, i):
        return jnp.where(tail, hi[i], lo[i])

    cap_code = [own(c_lo, c_hi, i) for i in range(LANES)]
    jam_code = [own(j_lo, j_hi, i) for i in range(LANES)]
    near = [own(a_lo, a_hi, i).astype(F32) for i in range(LANES - 1)]
    cap = [pick(x, cap_table, 8) for x in cap_code]
    jam = [pick(x, jam_table, 4) for x in jam_code]
    wave = [wave_of(c, j) for c, j in zip(cap, jam)]
    state = [[own(d_lo, d_hi, lane * CLASSES + k) for k in range(CLASSES)] for lane in range(LANES)]
    history = []
    for d in range(4):
        totals = [total_of(x) for x in state]
        supply = [supply_of(totals[i], cap[i], jam[i], wave[i]) for i in range(LANES)]
        ahead = [pltpu.roll(x, 7, 0) for x in supply]
        out = []
        for i in range(LANES):
            share = sent_share(totals[i], cap[i], ahead[i])
            out.append([x * share for x in state[i]])
        came = [[pltpu.roll(x, 1, 0) for x in row] for row in out]
        history.append((state, ahead, came))
        if d < 3:
            state = [
                [(state[i][k] + came[i][k]) - out[i][k] for k in range(CLASSES)]
                for i in range(LANES)
            ]
            state = lane_change(state, near, coef)
    codes = [x.astype(F32) for x in cap_code + jam_code] + near

    def put(row, value, at):
        zone[pl.ds(row, 1), :] = value[at : at + 1, :]

    @pl.when(tail)
    def _():
        for d in range(4):
            state, _, came = history[d]
            for i in range(LANES):
                for k in range(CLASSES):
                    put(TAIL_DEPTH * d + i * CLASSES + k, state[i][k], 7 - d)
                    put(TAIL_DEPTH * d + 12 + i * CLASSES + k, came[i][k], 7 - d)
            for n, x in enumerate(codes):
                put(TAIL_DEPTH * d + 24 + n, x, 7 - d)
        zone[pl.ds(FEED_ROW, 1), :] = feed_b_row[...].astype(F32)
        zone[pl.ds(SHARE_ROW, 1), :] = share_row[...]

    @pl.when(jnp.logical_not(tail))
    def _():
        for d in range(4):
            state, ahead, _ = history[d]
            for i in range(LANES):
                for k in range(CLASSES):
                    put(HEAD_DEPTH * d + i * CLASSES + k, state[i][k], d)
                put(HEAD_DEPTH * d + 12 + i, ahead[i], d)
            for n, x in enumerate(codes):
                put(HEAD_DEPTH * d + 16 + n, x, d)
        zone[pl.ds(RAMP_ROW, 32), :] = ramp[...].astype(F32)
        zone[pl.ds(FEED_ROW, 1), :] = feed_a_row[...].astype(F32)
        zone[pl.ds(SHARE_ROW, 1), :] = prio_row[...]

    index = lax.broadcasted_iota(jnp.int32, (8, WIDTH), 0) * WIDTH + lax.broadcasted_iota(
        jnp.int32, (8, WIDTH), 1
    )

    def note(c, found):
        feed = jnp.where(tail, feed_b[c], feed_a[c])
        return jnp.where(index == feed, place * WIDTH + c, found)

    found = lax.fori_loop(0, WIDTH, note, jnp.zeros((8, WIDTH), jnp.int32), unroll=16)
    zone[pl.ds(INVERSE_ROW, 8), :] = found.astype(F32)
    zone[pl.ds(INVERSE_ROW + 8, 2), :] = jnp.zeros((2, WIDTH), F32)


def inner_kernel(
    cap_table, jam_table, coef_ref, density, cap_code, jam_code, adjacency,
    traffic, acc_out, low, stats, st, tot, cap, jam, wave, adj, level, acc,
):
    coef = [coef_ref[k] for k in range(CLASSES)]
    fill(
        16, 16, (st, tot, cap, jam, wave, adj, level, acc),
        lambda i, rows: density[i, rows, :],
        lambda i, rows: cap_code[i, rows, :],
        lambda i, rows: jam_code[i, rows, :],
        lambda i, rows: adjacency[i, rows, :].astype(F32),
        cap_table, jam_table,
    )
    sub = lax.broadcasted_iota(jnp.int32, (8, WIDTH), 0)

    def one(step, carry):
        def scan(running, lowest):
            total, least = running, lowest
            for shift in (1, 2, 4):
                here = sub >= shift
                t = jnp.where(here, pltpu.roll(total, shift, 0), 0.0)
                m = jnp.where(here, pltpu.roll(least, shift, 0), BIG)
                least = jnp.minimum(m, t + least)
                total = t + total
            stats[0, pl.ds(step, 1), :] = total[7:8, :]
            stats[1, pl.ds(step, 1), :] = least[7:8, :]
            return (
                jnp.where(sub >= 1, pltpu.roll(total, 1, 0), 0.0),
                jnp.where(sub >= 1, pltpu.roll(least, 1, 0), BIG),
            )

        window(
            16, (st, tot, cap, jam, wave, adj, level, acc, low), step, coef,
            lambda v, before, leaving: (before, leaving),
            lambda v: (sub != 0) if v < 8 else (sub != 7),
            scan,
        )
        return carry

    lax.fori_loop(0, STEPS, one, 0)
    for v in range(16):
        for i in range(LANES * CLASSES):
            traffic[i, pl.ds(v, 8, stride=16), :] = st[i, v]
        acc_out[v] = acc[0, v]


def junctions(near_here, zone, inj, spare_rows, cap_table, jam_table, coef):
    head_row = lax.axis_index("corr") == 0

    def head(row):
        return zone[pl.ds(row * 8, 8), :]

    def tail(row):
        return zone[pl.ds((RECORD + row) * 8, 8), :]

    def whole(x):
        return x.astype(jnp.int32)

    feed_a = whole(head(FEED_ROW))
    feed_b = whole(tail(FEED_ROW))
    prio = head(SHARE_ROW)
    share = tail(SHARE_ROW)
    for side, read in enumerate((head, tail)):
        for i in range(8):
            spare_rows[pl.ds(side * 8 + i, 1), :] = jnp.sum(
                read(INVERSE_ROW + i), axis=0, keepdims=True
            )
    back_from_a = whole(spare_rows[pl.ds(0, 8), :])
    back_from_b = whole(spare_rows[pl.ds(8, 8), :])

    def plan(index):
        chunk = index // WIDTH
        lane = index - chunk * WIDTH
        return lane, [chunk == i for i in range(1, 8)]

    plan_a, plan_b, plan_ra, plan_rb = (
        plan(x) for x in (feed_a, feed_b, back_from_a, back_from_b)
    )

    def permute(x, how):
        lane, masks = how
        out = None
        for i in range(8):
            row = jnp.broadcast_to(x[i : i + 1, :], (8, WIDTH))
            got = jnp.take_along_axis(row, lane, axis=1, mode="promise_in_bounds")
            out = got if out is None else jnp.where(masks[i - 1], got, out)
        return out

    def statics(read, base):
        cap = [pick(whole(read(base + i)), cap_table, 8) for i in range(LANES)]
        jam = [pick(whole(read(base + 4 + i)), jam_table, 4) for i in range(LANES)]
        wave = [wave_of(c, j) for c, j in zip(cap, jam)]
        return cap, jam, wave, [read(base + 8 + p) for p in range(LANES - 1)]

    head_fixed = [statics(head, HEAD_DEPTH * d + 16) for d in range(4)]
    tail_fixed = [statics(tail, TAIL_DEPTH * d + 24) for d in range(4)]

    def first(read, base):
        return [[read(base + i * CLASSES + k) for k in range(CLASSES)] for i in range(LANES)]

    def supplies(state, fixed):
        return [
            supply_of(total_of(state[i]), fixed[0][i], fixed[1][i], fixed[2][i])
            for i in range(LANES)
        ]

    def fluxes(state, fixed, next_supply):
        out = []
        for i in range(LANES):
            q = sent_share(total_of(state[i]), fixed[0][i], next_supply[i])
            out.append([x * q for x in state[i]])
        return out

    heads, tails = {}, {}
    for step in range(STEPS):
        if step < 4:
            heads[step] = first(head, HEAD_DEPTH * step)
            tails[step] = first(tail, TAIL_DEPTH * step)
        deep = min(step, 6 - step)
        supply = supplies(heads[0], head_fixed[0])
        arriving, rates = [], []
        for i in range(LANES):
            state = tails[0][i]
            speed = jnp.minimum(0.5, tail_fixed[0][0][i] * inverse(total_of(state)))
            demand = [x * speed for x in state]
            part_a = [share * x for x in demand]
            part_b = [x - y for x, y in zip(demand, part_a)]
            take_a = [permute(x, plan_a) for x in part_a]
            take_b = [permute(x, plan_b) for x in part_b]
            need_a = total_of(take_a)
            need_b = total_of(take_b)
            s = supply[i]
            share_a = prio * s
            share_b = (1.0 - prio) * s
            pass_a = jnp.minimum(need_a, middle(need_a, s - need_b, share_a))
            pass_b = jnp.minimum(need_b, middle(need_b, s - need_a, share_b))
            rate_a = pass_a / need_a
            rate_b = pass_b / need_b
            ramp = jnp.minimum(
                head(RAMP_ROW + step * LANES + i) * RAMP_UNIT,
                jnp.maximum((s - pass_a) - pass_b, 0.0),
            )
            arriving.append(
                [
                    (take_a[k] * rate_a + take_b[k] * rate_b) + RAMP_FRACTION[k] * ramp
                    for k in range(CLASSES)
                ]
            )
            back_a = permute(rate_a, plan_ra)
            back_b = permute(rate_b, plan_rb)
            rates.append([part_a[k] * back_a + part_b[k] * back_b for k in range(CLASSES)])
        for i in range(LANES):
            for k in range(CLASSES):
                inj[pl.ds((step * 12 + i * CLASSES + k) * 8, 8), :] = jnp.where(
                    head_row, arriving[i][k], rates[i][k]
                )
        if step == STEPS - 1:
            break
        new_heads, new_tails = {}, {}
        came, gone = arriving, rates
        for d in range(deep + 1):
            if d < deep or deep < step:
                ahead = supplies(heads[d + 1], head_fixed[d + 1])
                entering = fluxes(tails[d + 1], tail_fixed[d + 1], supplies(tails[d], tail_fixed[d]))
            else:
                ahead = [head(HEAD_DEPTH * d + 12 + i) for i in range(LANES)]
                entering = first(tail, TAIL_DEPTH * d + 12)
            out = fluxes(heads[d], head_fixed[d], ahead)
            moved = [
                [(heads[d][i][k] + came[i][k]) - out[i][k] for k in range(CLASSES)]
                for i in range(LANES)
            ]
            new_heads[d] = lane_change(moved, head_fixed[d][3], coef)
            moved = [
                [(tails[d][i][k] + entering[i][k]) - gone[i][k] for k in range(CLASSES)]
                for i in range(LANES)
            ]
            new_tails[d] = lane_change(moved, tail_fixed[d][3], coef)
            came, gone = out, entering
        heads, tails = new_heads, new_tails


def edge_kernel(
    cap_table, jam_table, coef_ref, d_lo, d_hi, c_lo, c_hi, j_lo, j_hi, a_lo, a_hi, left, right,
    ends_here, ends_other, inner, traffic_in, traffic, segment, aux, acc_out, low,
    nat, zone, inj, spare_rows, st, tot, cap, jam, wave, adj, level, acc, out, sem,
):
    del traffic_in
    row = lax.axis_index("corr")
    place = lax.axis_index("lc")
    coef = [coef_ref[k] for k in range(CLASSES)]
    first_row = row == 0
    last_row = row == ROWS - 1

    @pl.when(jnp.logical_or(first_row, last_row))
    def _():
        for swap, ends in ((0, ends_here), (1, ends_other)):
            core = jnp.where(swap == 0, place % 2, 1 - place % 2)
            for z in range(4):
                for m in range(2):
                    side = jnp.where(first_row, m, 1 - m)
                    base = side * (RECORD * 8) + 2 * z + core
                    for r in range(RECORD // 8):
                        zone[pl.ds(base + r * 64, 8, stride=8), :] = ends[
                            z, pl.ds(m * RECORD + r * 8, 8), :
                        ]
        junctions(place, zone, inj, spare_rows, cap_table, jam_table, coef)

    index = 0
    for n, lo, hi in ((12, d_lo, d_hi), (4, c_lo, c_hi), (4, j_lo, j_hi), (3, a_lo, a_hi)):
        for i in range(n):
            base = index * 48
            nat[pl.ds(base, 8), :] = left[pl.ds(index * 8, 8), :]
            nat[pl.ds(base + 8, 16), :] = lo[i].astype(F32)
            nat[pl.ds(base + 24, 16), :] = hi[i].astype(F32)
            nat[pl.ds(base + 40, 8), :] = right[pl.ds(index * 8, 8), :]
            index += 1

    def rows_of(base):
        def read(i, rows):
            return nat[pl.ds((base + i) * 48 + rows.start, 8, stride=6), :]

        return read

    def code_of(base):
        read = rows_of(base)
        return lambda i, rows: read(i, rows).astype(jnp.int32)

    fill(
        6, 6, (st, tot, cap, jam, wave, adj, level, acc),
        rows_of(0), code_of(12), code_of(16), rows_of(20), cap_table, jam_table,
    )
    sub = lax.broadcasted_iota(jnp.int32, (8, WIDTH), 0)
    in_strip = sub % 4
    at_head = jnp.logical_and(sub == 1, first_row)
    at_tail = jnp.logical_and(sub == 6, last_row)

    def one(step, carry):
        def injected(i, k):
            return jnp.broadcast_to(
                inj[pl.ds((step * 12 + i * CLASSES + k) * 8 + place, 1), :], (8, WIDTH)
            )

        def inject(v, before, leaving):
            came, gone = before, leaving
            if v == 2:
                came = [
                    [jnp.where(at_head, injected(i, k), before[i][k]) for k in range(CLASSES)]
                    for i in range(LANES)
                ]
            if v == 3:
                gone = [
                    [jnp.where(at_tail, injected(i, k), leaving[i][k]) for k in range(CLASSES)]
                    for i in range(LANES)
                ]
            return came, gone

        def mask(v):
            if v < 2:
                return in_strip == 2
            if v < 4:
                return jnp.logical_or(in_strip == 1, in_strip == 2)
            return in_strip == 1

        def scan(running, lowest):
            second = in_strip == 2
            carry = jnp.where(second, pltpu.roll(running, 1, 0), 0.0)
            floor = jnp.where(second, pltpu.roll(lowest, 1, 0), BIG)
            total = carry + running
            least = jnp.minimum(floor, carry + lowest)
            aux[0, pl.ds(step, 1), :] = total[2:3, :]
            aux[1, pl.ds(step, 1), :] = least[2:3, :]
            aux[2, pl.ds(step, 1), :] = total[6:7, :]
            aux[3, pl.ds(step, 1), :] = least[6:7, :]
            return carry, floor

        window(
            6, (st, tot, cap, jam, wave, adj, level, acc, low), step, coef, inject, mask, scan
        )
        return carry

    lax.fori_loop(0, STEPS, one, 0)
    for v in range(6):
        for i in range(LANES * CLASSES):
            nat[pl.ds(i * 48 + v, 8, stride=6), :] = st[i, v]
        acc_out[v] = acc[0, v]
    for i in range(LANES * CLASSES):
        out[0, i] = nat[pl.ds(i * 48 + 8, 8), :]
        out[1, i] = nat[pl.ds(i * 48 + 32, 8), :]
    copies = [
        pltpu.make_async_copy(out.at[0], traffic.at[:, pl.ds(0, 8), :], sem.at[0]),
        pltpu.make_async_copy(out.at[1], traffic.at[:, pl.ds(CELLS_HERE - 8, 8), :], sem.at[1]),
    ]
    for copy in copies:
        copy.start()
    left_sum, left_low = aux[0], aux[1]
    most_sum = left_sum + inner[0]
    most_low = jnp.minimum(left_low, left_sum + inner[1])
    all_sum = most_sum + aux[2]
    all_low = jnp.minimum(most_low, most_sum + aux[3])
    for i in range(ROWS):
        segment[i, 0] = all_sum
        segment[i, 1] = all_low
    for copy in copies:
        copy.wait()


def count_kernel(
    segments, aux, inner, acc, low, edge_acc, edge_low, queue, sums, floors, nat
):
    row = lax.axis_index("corr")
    total = jnp.zeros((8, WIDTH), F32)
    least = jnp.zeros((8, WIDTH), F32)
    for i in range(ROWS - 1):
        on = i < row
        least = jnp.where(on, jnp.minimum(least, total + segments[i, 1]), least)
        total = jnp.where(on, total + segments[i, 0], total)
    mid_total = total + aux[0]
    mid_least = jnp.minimum(least, total + aux[1])
    end_total = mid_total + inner[0]
    end_least = jnp.minimum(mid_least, mid_total + inner[1])
    for n, (t, m) in enumerate(((total, least), (mid_total, mid_least), (end_total, end_least))):
        sums[n] = t
        floors[n] = m
    scale = 1.0 / (STEPS * CELLS_HERE * ROWS)
    left = lax.broadcasted_iota(jnp.int32, (8, WIDTH), 0) < 4

    def spread(ref, n, step):
        return jnp.broadcast_to(ref[n, pl.ds(step, 1), :], (8, WIDTH))

    inside = [(spread(sums, 1, s), spread(floors, 1, s)) for s in range(STEPS)]
    for v in range(16):
        value = acc[v]
        for s in range(STEPS):
            value = value + (inside[s][0] - jnp.minimum(inside[s][1], inside[s][0] + low[s, v]))
        queue[pl.ds(v, 8, stride=16), :] = value * scale
    edges = [
        (
            jnp.where(left, spread(sums, 0, s), spread(sums, 2, s)),
            jnp.where(left, spread(floors, 0, s), spread(floors, 2, s)),
        )
        for s in range(STEPS)
    ]
    for v in range(6):
        value = edge_acc[v]
        for s in range(STEPS):
            value = value + (edges[s][0] - jnp.minimum(edges[s][1], edges[s][0] + edge_low[s, v]))
        nat[pl.ds(v, 8, stride=6), :] = value * scale
    queue[pl.ds(0, 8), :] = nat[pl.ds(8, 8), :]
    queue[pl.ds(CELLS_HERE - 8, 8), :] = nat[pl.ds(32, 8), :]


def shape(*dims):
    return jax.ShapeDtypeStruct(dims, F32)


def full(*dims):
    return pl.BlockSpec(dims, lambda i: (0,) * len(dims))


def part(place, *dims):
    return pl.BlockSpec(dims, lambda i: (0, place, 0))


SCALARS = pl.BlockSpec(memory_space=pltpu.SMEM)


def call(kernel, name, args, in_specs, outs, out_specs, scratch=(), aliases=None, flops=0):
    return pl.pallas_call(
        kernel,
        grid=(1,),
        in_specs=in_specs,
        out_specs=out_specs,
        out_shape=outs,
        scratch_shapes=scratch,
        input_output_aliases=aliases or {},
        compiler_params=pltpu.CompilerParams(vmem_limit_bytes=VMEM_BYTES),
        cost_estimate=pl.CostEstimate(flops=flops, bytes_accessed=4 << 20, transcendentals=0),
        name=name,
    )(*args)


def cells_scratch(count):
    def hold(n):
        return pltpu.VMEM((n, count, 8, WIDTH), F32)

    return [hold(12), hold(4), hold(4), hold(4), hold(4), hold(3), pltpu.VMEM((count, 8, WIDTH), F32), hold(2)]


def on_device(
    density, cap_code, jam_code, adjacency, ramp_code, feed_a, feed_b, turn_share, priority,
    cap_table, jam_table, change_coef,
):
    density = density.reshape(12, CELLS_HERE, WIDTH)
    tables = [cap_table, jam_table, change_coef]
    grids = [density, cap_code, jam_code, adjacency]
    sizes = (12, 4, 4, 3)

    def ends(depth):
        args, specs = [], []
        for x, n in zip(grids, sizes):
            args += [x, x]
            specs += [part(0, n, depth, WIDTH), part(CELLS_HERE // depth - 1, n, depth, WIDTH)]
        return args, specs

    args, specs = ends(8)
    line = [x.reshape(1, WIDTH) for x in (feed_a, feed_b, turn_share, priority)]
    fwd, bwd, record = call(
        pack_kernel, "pack",
        tables + [feed_a, feed_b] + line + [ramp_code.reshape(32, WIDTH)] + args,
        [SCALARS] * 5 + [full(1, WIDTH)] * 4 + [full(32, WIDTH)] + specs,
        [shape(184, WIDTH), shape(184, WIDTH), shape(RECORD, WIDTH)],
        [full(184, WIDTH), full(184, WIDTH), full(RECORD, WIDTH)],
    )
    other_end = lax.ppermute(record, "corr", [(0, ROWS - 1), (ROWS - 1, 0)])
    left = lax.ppermute(fwd, "corr", [(i, i + 1) for i in range(ROWS - 1)])
    right = lax.ppermute(bwd, "corr", [(i + 1, i) for i in range(ROWS - 1)])
    traffic, acc, low, inner = call(
        inner_kernel, "inner", tables + grids,
        [SCALARS] * 3 + [full(n, CELLS_HERE, WIDTH) for n in sizes],
        [shape(12, CELLS_HERE, WIDTH), shape(16, 8, WIDTH), shape(8, 16, 8, WIDTH), shape(2, 8, WIDTH)],
        [full(12, CELLS_HERE, WIDTH), full(16, 8, WIDTH), full(8, 16, 8, WIDTH), full(2, 8, WIDTH)],
        cells_scratch(16),
        flops=1 << 27,
    )
    both = jnp.concatenate([record, other_end], 0)
    ends_here = lax.all_gather(
        both, "lc", axis_index_groups=[[0, 2, 4, 6], [1, 3, 5, 7]]
    )
    ends_other = lax.ppermute(ends_here, "lc", [(i, i ^ 1) for i in range(8)])
    args, specs = ends(16)
    any_space = pl.BlockSpec(memory_space=pl.ANY)
    traffic, segment, aux, edge_acc, edge_low = call(
        edge_kernel, "edges",
        tables + args + [left, right, ends_here, ends_other, inner, traffic],
        [SCALARS] * 3 + specs + [full(184, WIDTH)] * 2 + [full(4, 2 * RECORD, WIDTH)] * 2
        + [full(2, 8, WIDTH), any_space],
        [shape(12, CELLS_HERE, WIDTH), shape(ROWS, 2, 8, WIDTH), shape(4, 8, WIDTH),
         shape(6, 8, WIDTH), shape(8, 6, 8, WIDTH)],
        [any_space, full(ROWS, 2, 8, WIDTH), full(4, 8, WIDTH), full(6, 8, WIDTH),
         full(8, 6, 8, WIDTH)],
        [pltpu.VMEM((23 * 48, WIDTH), F32), pltpu.VMEM((2 * RECORD * 8, WIDTH), F32),
         pltpu.VMEM((STEPS * 12 * 8, WIDTH), F32), pltpu.VMEM((16, WIDTH), F32)]
        + cells_scratch(6)
        + [pltpu.VMEM((2, 12, 8, WIDTH), F32), pltpu.SemaphoreType.DMA((2,))],
        aliases={16: 0},
    )
    segments = lax.all_to_all(segment, "corr", 0, 0)
    queue = call(
        count_kernel, "count", [segments, aux, inner, acc, low, edge_acc, edge_low],
        [full(ROWS, 2, 8, WIDTH), full(4, 8, WIDTH), full(2, 8, WIDTH), full(16, 8, WIDTH),
         full(8, 16, 8, WIDTH), full(6, 8, WIDTH), full(8, 6, 8, WIDTH)],
        shape(CELLS_HERE, WIDTH), full(CELLS_HERE, WIDTH),
        [pltpu.VMEM((3, 8, WIDTH), F32), pltpu.VMEM((3, 8, WIDTH), F32), pltpu.VMEM((48, WIDTH), F32)],
    )
    return traffic.reshape(LANES, CLASSES, CELLS_HERE, WIDTH), queue


def solution(mesh):
    placed = (
        P(None, None, "corr", "lc"),
        P(None, "corr", "lc"),
        P(None, "corr", "lc"),
        P(None, "corr", "lc"),
        P(None, None, "lc"),
        P("lc"),
        P("lc"),
        P("lc"),
        P("lc"),
        P(),
        P(),
        P(),
    )
    return jax.shard_map(
        on_device,
        mesh=mesh,
        in_specs=placed,
        out_specs=(P(None, None, "corr", "lc"), P("corr", "lc")),
        check_vma=False,
    )
```

```python
import jax
import jax.numpy as jnp
from jax import lax
from jax.experimental import pallas as pl
from jax.experimental.pallas import tpu as pltpu
from jax.sharding import PartitionSpec as P

STEPS = 8
LANES = 4
CLASSES = 3
ROWS = 16
WIDTH = 128
CELLS_HERE = 128
BIG = 1e30
F32 = jnp.float32
RAMP_UNIT = 0.01
RAMP_FRACTION = (0.56, 0.16, 0.08)

HEAD_DEPTH = 27
TAIL_DEPTH = 35
RAMP_ROW = 108
FEED_ROW = 140
SHARE_ROW = 141
INVERSE_ROW = 142
RECORD = 152


def inverse(x):
    r = pl.reciprocal(x, approx=True)
    return r * (2.0 - x * r)


def total_of(state):
    return state[0] + 1.5 * state[1] + 2.5 * state[2]


def supply_of(totals, cap, jam, wave):
    return jnp.maximum(jnp.minimum(cap, wave * (jam - totals)), 0.0)


def sent_share(totals, cap, next_supply):
    return jnp.minimum(0.5, jnp.minimum(cap, next_supply) * inverse(totals))


def pick(code, table, count):
    values = [table[i] for i in range(count)]
    bit = 1
    while len(values) > 1:
        on = (code & bit) != 0
        values = [jnp.where(on, values[i + 1], values[i]) for i in range(0, len(values), 2)]
        bit *= 2
    return values[0]


def wave_of(cap, jam):
    return cap / (jam - 2.0 * cap)


def lane_change(state, adjacent, coef):
    moving = [
        [(adjacent[p] * coef[k]) * (state[p][k] - state[p + 1][k]) for k in range(CLASSES)]
        for p in range(LANES - 1)
    ]
    out = []
    for lane in range(LANES):
        row = []
        for k in range(CLASSES):
            value = state[lane][k]
            if lane < LANES - 1:
                value = value - moving[lane][k]
            if lane > 0:
                value = value + moving[lane - 1][k]
            row.append(value)
        out.append(row)
    return out


def middle(a, b, c):
    return jnp.maximum(jnp.minimum(a, b), jnp.minimum(jnp.maximum(a, b), c))


def window(count, refs, step, coef, inject, mask, scan):
    st, tot, cap, jam, wave, adj, level, acc, low = refs
    last = count - 1

    def supply(v):
        return [
            supply_of(tot[lane, v], cap[lane, v], jam[lane, v], wave[lane, v])
            for lane in range(LANES)
        ]

    def flux(v, next_supply):
        out = []
        for lane in range(LANES):
            share = sent_share(tot[lane, v], cap[lane, v], next_supply[lane])
            out.append([st[lane * CLASSES + k, v] * share for k in range(CLASSES)])
        return out

    wrapped = [pltpu.roll(x, 7, 0) for x in supply(0)]
    final = flux(last, wrapped)
    before = [[pltpu.roll(x, 1, 0) for x in row] for row in final]
    running = lowest = None
    for v in range(count):
        leaving = flux(v, supply(v + 1)) if v < last else final
        came, gone = inject(v, before, leaving)
        state = [
            [(st[lane * CLASSES + k, v] + came[lane][k]) - gone[lane][k] for k in range(CLASSES)]
            for lane in range(LANES)
        ]
        state = lane_change(state, [adj[p, v] for p in range(LANES - 1)], coef)
        sums = []
        for lane in range(LANES):
            for k in range(CLASSES):
                st[lane * CLASSES + k, v] = state[lane][k]
            sums.append(total_of(state[lane]))
            tot[lane, v] = sums[lane]
        excess = 0.25 * ((sums[0] + sums[1]) + (sums[2] + sums[3])) - level[v]
        excess = jnp.where(mask(v), excess, 0.0)
        running = excess if running is None else running + excess
        lowest = running if lowest is None else jnp.minimum(lowest, running)
        acc[1, v] = running
        low[step, v] = lowest
        before = leaving
    carry, floor = scan(running, lowest)
    for v in range(count):
        acc[0, v] = acc[0, v] + (carry + acc[1, v])
        low[step, v] = jnp.minimum(floor, carry + low[step, v])


def fill(count, stride, refs, density, cap_code, jam_code, adjacency, cap_table, jam_table):
    st, tot, cap, jam, wave, adj, level, acc = refs
    for v in range(count):
        rows = pl.ds(v, 8, stride=stride)
        around = None
        for lane in range(LANES):
            state = [density(lane * CLASSES + k, rows) for k in range(CLASSES)]
            for k in range(CLASSES):
                st[lane * CLASSES + k, v] = state[k]
            tot[lane, v] = total_of(state)
            c = pick(cap_code(lane, rows), cap_table, 8)
            j = pick(jam_code(lane, rows), jam_table, 4)
            cap[lane, v] = c
            jam[lane, v] = j
            wave[lane, v] = wave_of(c, j)
            around = c if around is None else around + c
        for p in range(LANES - 1):
            adj[p, v] = adjacency(p, rows)
        level[v] = 0.5 * around
        acc[0, v] = jnp.zeros((8, WIDTH), F32)


def pack_kernel(
    cap_table, jam_table, coef_ref, feed_a, feed_b, feed_a_row, feed_b_row, share_row, prio_row,
    ramp, d_lo, d_hi, c_lo, c_hi, j_lo, j_hi, a_lo, a_hi, fwd, bwd, zone,
):
    row_here = lax.axis_index("corr")
    tail = row_here == ROWS - 1
    place = lax.axis_index("lc")
    for out, d, c, j, a in ((bwd, d_lo, c_lo, j_lo, a_lo), (fwd, d_hi, c_hi, j_hi, a_hi)):
        row = 0
        for ref, n in ((d, 12), (c, 4), (j, 4), (a, 3)):
            for i in range(n):
                out[pl.ds(row * 8, 8), :] = ref[i].astype(F32)
                row += 1
    coef = [coef_ref[k] for k in range(CLASSES)]

    def own(lo, hi, i):
        return jnp.where(tail, hi[i], lo[i])

    cap_code = [own(c_lo, c_hi, i) for i in range(LANES)]
    jam_code = [own(j_lo, j_hi, i) for i in range(LANES)]
    near = [own(a_lo, a_hi, i).astype(F32) for i in range(LANES - 1)]
    cap = [pick(x, cap_table, 8) for x in cap_code]
    jam = [pick(x, jam_table, 4) for x in jam_code]
    wave = [wave_of(c, j) for c, j in zip(cap, jam)]
    state = [[own(d_lo, d_hi, lane * CLASSES + k) for k in range(CLASSES)] for lane in range(LANES)]
    history = []
    for d in range(4):
        totals = [total_of(x) for x in state]
        supply = [supply_of(totals[i], cap[i], jam[i], wave[i]) for i in range(LANES)]
        ahead = [pltpu.roll(x, 7, 0) for x in supply]
        out = []
        for i in range(LANES):
            share = sent_share(totals[i], cap[i], ahead[i])
            out.append([x * share for x in state[i]])
        came = [[pltpu.roll(x, 1, 0) for x in row] for row in out]
        history.append((state, ahead, came))
        if d < 3:
            state = [
                [(state[i][k] + came[i][k]) - out[i][k] for k in range(CLASSES)]
                for i in range(LANES)
            ]
            state = lane_change(state, near, coef)
    codes = [x.astype(F32) for x in cap_code + jam_code] + near

    def put(row, value, at):
        zone[pl.ds(row, 1), :] = value[at : at + 1, :]

    @pl.when(tail)
    def _():
        for d in range(4):
            state, _, came = history[d]
            for i in range(LANES):
                for k in range(CLASSES):
                    put(TAIL_DEPTH * d + i * CLASSES + k, state[i][k], 7 - d)
                    put(TAIL_DEPTH * d + 12 + i * CLASSES + k, came[i][k], 7 - d)
            for n, x in enumerate(codes):
                put(TAIL_DEPTH * d + 24 + n, x, 7 - d)
        zone[pl.ds(FEED_ROW, 1), :] = feed_b_row[...].astype(F32)
        zone[pl.ds(SHARE_ROW, 1), :] = share_row[...]

    @pl.when(jnp.logical_not(tail))
    def _():
        for d in range(4):
            state, ahead, _ = history[d]
            for i in range(LANES):
                for k in range(CLASSES):
                    put(HEAD_DEPTH * d + i * CLASSES + k, state[i][k], d)
                put(HEAD_DEPTH * d + 12 + i, ahead[i], d)
            for n, x in enumerate(codes):
                put(HEAD_DEPTH * d + 16 + n, x, d)
        zone[pl.ds(RAMP_ROW, 32), :] = ramp[...].astype(F32)
        zone[pl.ds(FEED_ROW, 1), :] = feed_a_row[...].astype(F32)
        zone[pl.ds(SHARE_ROW, 1), :] = prio_row[...]

    index = lax.broadcasted_iota(jnp.int32, (8, WIDTH), 0) * WIDTH + lax.broadcasted_iota(
        jnp.int32, (8, WIDTH), 1
    )

    def note(c, found):
        feed = jnp.where(tail, feed_b[c], feed_a[c])
        return jnp.where(index == feed, place * WIDTH + c, found)

    found = lax.fori_loop(0, WIDTH, note, jnp.zeros((8, WIDTH), jnp.int32), unroll=16)
    zone[pl.ds(INVERSE_ROW, 8), :] = found.astype(F32)
    zone[pl.ds(INVERSE_ROW + 8, 2), :] = jnp.zeros((2, WIDTH), F32)

    @pl.when(tail)
    def _():
        fwd[pl.ds(0, RECORD), :] = zone[...]

    @pl.when(row_here == 0)
    def _():
        bwd[pl.ds(0, RECORD), :] = zone[...]


def inner_kernel(
    cap_table, jam_table, coef_ref, density, cap_code, jam_code, adjacency,
    traffic, acc_out, low, stats, st, tot, cap, jam, wave, adj, level, acc,
):
    coef = [coef_ref[k] for k in range(CLASSES)]
    fill(
        16, 16, (st, tot, cap, jam, wave, adj, level, acc),
        lambda i, rows: density[i, rows, :],
        lambda i, rows: cap_code[i, rows, :],
        lambda i, rows: jam_code[i, rows, :],
        lambda i, rows: adjacency[i, rows, :].astype(F32),
        cap_table, jam_table,
    )
    sub = lax.broadcasted_iota(jnp.int32, (8, WIDTH), 0)

    def one(step, carry):
        def scan(running, lowest):
            total, least = running, lowest
            for shift in (1, 2, 4):
                here = sub >= shift
                t = jnp.where(here, pltpu.roll(total, shift, 0), 0.0)
                m = jnp.where(here, pltpu.roll(least, shift, 0), BIG)
                least = jnp.minimum(m, t + least)
                total = t + total
            stats[0, pl.ds(step, 1), :] = total[7:8, :]
            stats[1, pl.ds(step, 1), :] = least[7:8, :]
            return (
                jnp.where(sub >= 1, pltpu.roll(total, 1, 0), 0.0),
                jnp.where(sub >= 1, pltpu.roll(least, 1, 0), BIG),
            )

        window(
            16, (st, tot, cap, jam, wave, adj, level, acc, low), step, coef,
            lambda v, before, leaving: (before, leaving),
            lambda v: (sub != 0) if v < 8 else (sub != 7),
            scan,
        )
        return carry

    lax.fori_loop(0, STEPS, one, 0)
    for v in range(16):
        for i in range(LANES * CLASSES):
            traffic[i, pl.ds(v, 8, stride=16), :] = st[i, v]
        acc_out[v] = acc[0, v]


def junctions(near_here, zone, inj, spare_rows, cap_table, jam_table, coef):
    head_row = lax.axis_index("corr") == 0

    def head(row):
        return zone[pl.ds(row * 8, 8), :]

    def tail(row):
        return zone[pl.ds((RECORD + row) * 8, 8), :]

    def whole(x):
        return x.astype(jnp.int32)

    feed_a = whole(head(FEED_ROW))
    feed_b = whole(tail(FEED_ROW))
    prio = head(SHARE_ROW)
    share = tail(SHARE_ROW)
    for side, read in enumerate((head, tail)):
        for i in range(8):
            spare_rows[pl.ds(side * 8 + i, 1), :] = jnp.sum(
                read(INVERSE_ROW + i), axis=0, keepdims=True
            )
    back_from_a = whole(spare_rows[pl.ds(0, 8), :])
    back_from_b = whole(spare_rows[pl.ds(8, 8), :])

    def plan(index):
        chunk = index // WIDTH
        lane = index - chunk * WIDTH
        return lane, [chunk == i for i in range(1, 8)]

    plan_a, plan_b, plan_ra, plan_rb = (
        plan(x) for x in (feed_a, feed_b, back_from_a, back_from_b)
    )

    def permute(x, how):
        lane, masks = how
        out = None
        for i in range(8):
            row = jnp.broadcast_to(x[i : i + 1, :], (8, WIDTH))
            got = jnp.take_along_axis(row, lane, axis=1, mode="promise_in_bounds")
            out = got if out is None else jnp.where(masks[i - 1], got, out)
        return out

    def statics(read, base):
        cap = [pick(whole(read(base + i)), cap_table, 8) for i in range(LANES)]
        jam = [pick(whole(read(base + 4 + i)), jam_table, 4) for i in range(LANES)]
        wave = [wave_of(c, j) for c, j in zip(cap, jam)]
        return cap, jam, wave, [read(base + 8 + p) for p in range(LANES - 1)]

    head_fixed = [statics(head, HEAD_DEPTH * d + 16) for d in range(4)]
    tail_fixed = [statics(tail, TAIL_DEPTH * d + 24) for d in range(4)]

    def first(read, base):
        return [[read(base + i * CLASSES + k) for k in range(CLASSES)] for i in range(LANES)]

    def supplies(state, fixed):
        return [
            supply_of(total_of(state[i]), fixed[0][i], fixed[1][i], fixed[2][i])
            for i in range(LANES)
        ]

    def fluxes(state, fixed, next_supply):
        out = []
        for i in range(LANES):
            q = sent_share(total_of(state[i]), fixed[0][i], next_supply[i])
            out.append([x * q for x in state[i]])
        return out

    heads, tails = {}, {}
    for step in range(STEPS):
        if step < 4:
            heads[step] = first(head, HEAD_DEPTH * step)
            tails[step] = first(tail, TAIL_DEPTH * step)
        deep = min(step, 6 - step)
        supply = supplies(heads[0], head_fixed[0])
        arriving, rates = [], []
        for i in range(LANES):
            state = tails[0][i]
            speed = jnp.minimum(0.5, tail_fixed[0][0][i] * inverse(total_of(state)))
            demand = [x * speed for x in state]
            part_a = [share * x for x in demand]
            part_b = [x - y for x, y in zip(demand, part_a)]
            take_a = [permute(x, plan_a) for x in part_a]
            take_b = [permute(x, plan_b) for x in part_b]
            need_a = total_of(take_a)
            need_b = total_of(take_b)
            s = supply[i]
            share_a = prio * s
            share_b = (1.0 - prio) * s
            pass_a = jnp.minimum(need_a, middle(need_a, s - need_b, share_a))
            pass_b = jnp.minimum(need_b, middle(need_b, s - need_a, share_b))
            rate_a = pass_a / need_a
            rate_b = pass_b / need_b
            ramp = jnp.minimum(
                head(RAMP_ROW + step * LANES + i) * RAMP_UNIT,
                jnp.maximum((s - pass_a) - pass_b, 0.0),
            )
            arriving.append(
                [
                    (take_a[k] * rate_a + take_b[k] * rate_b) + RAMP_FRACTION[k] * ramp
                    for k in range(CLASSES)
                ]
            )
            back_a = permute(rate_a, plan_ra)
            back_b = permute(rate_b, plan_rb)
            rates.append([part_a[k] * back_a + part_b[k] * back_b for k in range(CLASSES)])
        for i in range(LANES):
            for k in range(CLASSES):
                inj[pl.ds((step * 12 + i * CLASSES + k) * 8, 8), :] = jnp.where(
                    head_row, arriving[i][k], rates[i][k]
                )
        if step == STEPS - 1:
            break
        new_heads, new_tails = {}, {}
        came, gone = arriving, rates
        for d in range(deep + 1):
            if d < deep or deep < step:
                ahead = supplies(heads[d + 1], head_fixed[d + 1])
                entering = fluxes(tails[d + 1], tail_fixed[d + 1], supplies(tails[d], tail_fixed[d]))
            else:
                ahead = [head(HEAD_DEPTH * d + 12 + i) for i in range(LANES)]
                entering = first(tail, TAIL_DEPTH * d + 12)
            out = fluxes(heads[d], head_fixed[d], ahead)
            moved = [
                [(heads[d][i][k] + came[i][k]) - out[i][k] for k in range(CLASSES)]
                for i in range(LANES)
            ]
            new_heads[d] = lane_change(moved, head_fixed[d][3], coef)
            moved = [
                [(tails[d][i][k] + entering[i][k]) - gone[i][k] for k in range(CLASSES)]
                for i in range(LANES)
            ]
            new_tails[d] = lane_change(moved, tail_fixed[d][3], coef)
            came, gone = out, entering
        heads, tails = new_heads, new_tails


def edge_kernel(
    cap_table, jam_table, coef_ref, d_lo, d_hi, c_lo, c_hi, j_lo, j_hi, a_lo, a_hi, left, right,
    e0, e1, e2, e3, e4, e5, e6, e7, inner, traffic_in, traffic, segment, aux, acc_out, low,
    nat, zone, inj, spare_rows, st, tot, cap, jam, wave, adj, level, acc, out, sem,
):
    del traffic_in
    row = lax.axis_index("corr")
    place = lax.axis_index("lc")
    coef = [coef_ref[k] for k in range(CLASSES)]
    first_row = row == 0
    last_row = row == ROWS - 1

    @pl.when(jnp.logical_or(first_row, last_row))
    def _():
        for n, ends in enumerate((e0, e1, e2, e3, e4, e5, e6, e7)):
            chip = (place // 2 + (4 - n % 4)) % 4
            core = place % 2 if n < 4 else 1 - place % 2
            for m in range(2):
                side = jnp.where(first_row, m, 1 - m)
                base = side * (RECORD * 8) + 2 * chip + core
                for r in range(RECORD // 8):
                    zone[pl.ds(base + r * 64, 8, stride=8), :] = ends[
                        pl.ds(m * RECORD + r * 8, 8), :
                    ]
        junctions(place, zone, inj, spare_rows, cap_table, jam_table, coef)

    index = 0
    for n, lo, hi in ((12, d_lo, d_hi), (4, c_lo, c_hi), (4, j_lo, j_hi), (3, a_lo, a_hi)):
        for i in range(n):
            base = index * 48
            nat[pl.ds(base, 8), :] = left[pl.ds(index * 8, 8), :]
            nat[pl.ds(base + 8, 16), :] = lo[i].astype(F32)
            nat[pl.ds(base + 24, 16), :] = hi[i].astype(F32)
            nat[pl.ds(base + 40, 8), :] = right[pl.ds(index * 8, 8), :]
            index += 1

    def rows_of(base):
        def read(i, rows):
            return nat[pl.ds((base + i) * 48 + rows.start, 8, stride=6), :]

        return read

    def code_of(base):
        read = rows_of(base)
        return lambda i, rows: read(i, rows).astype(jnp.int32)

    fill(
        6, 6, (st, tot, cap, jam, wave, adj, level, acc),
        rows_of(0), code_of(12), code_of(16), rows_of(20), cap_table, jam_table,
    )
    sub = lax.broadcasted_iota(jnp.int32, (8, WIDTH), 0)
    in_strip = sub % 4
    at_head = jnp.logical_and(sub == 1, first_row)
    at_tail = jnp.logical_and(sub == 6, last_row)

    def one(step, carry):
        def injected(i, k):
            return jnp.broadcast_to(
                inj[pl.ds((step * 12 + i * CLASSES + k) * 8 + place, 1), :], (8, WIDTH)
            )

        def inject(v, before, leaving):
            came, gone = before, leaving
            if v == 2:
                came = [
                    [jnp.where(at_head, injected(i, k), before[i][k]) for k in range(CLASSES)]
                    for i in range(LANES)
                ]
            if v == 3:
                gone = [
                    [jnp.where(at_tail, injected(i, k), leaving[i][k]) for k in range(CLASSES)]
                    for i in range(LANES)
                ]
            return came, gone

        def mask(v):
            if v < 2:
                return in_strip == 2
            if v < 4:
                return jnp.logical_or(in_strip == 1, in_strip == 2)
            return in_strip == 1

        def scan(running, lowest):
            second = in_strip == 2
            carry = jnp.where(second, pltpu.roll(running, 1, 0), 0.0)
            floor = jnp.where(second, pltpu.roll(lowest, 1, 0), BIG)
            total = carry + running
            least = jnp.minimum(floor, carry + lowest)
            aux[0, pl.ds(step, 1), :] = total[2:3, :]
            aux[1, pl.ds(step, 1), :] = least[2:3, :]
            aux[2, pl.ds(step, 1), :] = total[6:7, :]
            aux[3, pl.ds(step, 1), :] = least[6:7, :]
            return carry, floor

        window(
            6, (st, tot, cap, jam, wave, adj, level, acc, low), step, coef, inject, mask, scan
        )
        return carry

    lax.fori_loop(0, STEPS, one, 0)
    for v in range(6):
        for i in range(LANES * CLASSES):
            nat[pl.ds(i * 48 + v, 8, stride=6), :] = st[i, v]
        acc_out[v] = acc[0, v]
    for i in range(LANES * CLASSES):
        out[0, i] = nat[pl.ds(i * 48 + 8, 8), :]
        out[1, i] = nat[pl.ds(i * 48 + 32, 8), :]
    copies = [
        pltpu.make_async_copy(out.at[0], traffic.at[:, pl.ds(0, 8), :], sem.at[0]),
        pltpu.make_async_copy(out.at[1], traffic.at[:, pl.ds(CELLS_HERE - 8, 8), :], sem.at[1]),
    ]
    for copy in copies:
        copy.start()
    left_sum, left_low = aux[0], aux[1]
    most_sum = left_sum + inner[0]
    most_low = jnp.minimum(left_low, left_sum + inner[1])
    all_sum = most_sum + aux[2]
    all_low = jnp.minimum(most_low, most_sum + aux[3])
    for i in range(ROWS):
        segment[i, 0] = all_sum
        segment[i, 1] = all_low
    for copy in copies:
        copy.wait()


def count_kernel(
    segments, aux, inner, acc, low, edge_acc, edge_low, queue, sums, floors, nat
):
    row = lax.axis_index("corr")
    total = jnp.zeros((8, WIDTH), F32)
    least = jnp.zeros((8, WIDTH), F32)
    for i in range(ROWS - 1):
        on = i < row
        least = jnp.where(on, jnp.minimum(least, total + segments[i, 1]), least)
        total = jnp.where(on, total + segments[i, 0], total)
    mid_total = total + aux[0]
    mid_least = jnp.minimum(least, total + aux[1])
    end_total = mid_total + inner[0]
    end_least = jnp.minimum(mid_least, mid_total + inner[1])
    for n, (t, m) in enumerate(((total, least), (mid_total, mid_least), (end_total, end_least))):
        sums[n] = t
        floors[n] = m
    scale = 1.0 / (STEPS * CELLS_HERE * ROWS)
    left = lax.broadcasted_iota(jnp.int32, (8, WIDTH), 0) < 4

    def spread(ref, n, step):
        return jnp.broadcast_to(ref[n, pl.ds(step, 1), :], (8, WIDTH))

    inside = [(spread(sums, 1, s), spread(floors, 1, s)) for s in range(STEPS)]
    for v in range(16):
        value = acc[v]
        for s in range(STEPS):
            value = value + (inside[s][0] - jnp.minimum(inside[s][1], inside[s][0] + low[s, v]))
        queue[pl.ds(v, 8, stride=16), :] = value * scale
    edges = [
        (
            jnp.where(left, spread(sums, 0, s), spread(sums, 2, s)),
            jnp.where(left, spread(floors, 0, s), spread(floors, 2, s)),
        )
        for s in range(STEPS)
    ]
    for v in range(6):
        value = edge_acc[v]
        for s in range(STEPS):
            value = value + (edges[s][0] - jnp.minimum(edges[s][1], edges[s][0] + edge_low[s, v]))
        nat[pl.ds(v, 8, stride=6), :] = value * scale
    queue[pl.ds(0, 8), :] = nat[pl.ds(8, 8), :]
    queue[pl.ds(CELLS_HERE - 8, 8), :] = nat[pl.ds(32, 8), :]


def shape(*dims):
    return jax.ShapeDtypeStruct(dims, F32)


def full(*dims):
    return pl.BlockSpec(dims, lambda i: (0,) * len(dims))


def part(place, *dims):
    return pl.BlockSpec(dims, lambda i: (0, place, 0))


SCALARS = pl.BlockSpec(memory_space=pltpu.SMEM)


def call(kernel, name, args, in_specs, outs, out_specs, scratch=(), aliases=None, flops=0, vmem=32):
    return pl.pallas_call(
        kernel,
        grid=(1,),
        in_specs=in_specs,
        out_specs=out_specs,
        out_shape=outs,
        scratch_shapes=scratch,
        input_output_aliases=aliases or {},
        compiler_params=pltpu.CompilerParams(vmem_limit_bytes=vmem << 20),
        cost_estimate=pl.CostEstimate(flops=flops, bytes_accessed=4 << 20, transcendentals=0),
        name=name,
    )(*args)


def cells_scratch(count):
    def hold(n):
        return pltpu.VMEM((n, count, 8, WIDTH), F32)

    return [hold(12), hold(4), hold(4), hold(4), hold(4), hold(3), pltpu.VMEM((count, 8, WIDTH), F32), hold(2)]


def on_device(
    density, cap_code, jam_code, adjacency, ramp_code, feed_a, feed_b, turn_share, priority,
    cap_table, jam_table, change_coef,
):
    density = density.reshape(12, CELLS_HERE, WIDTH)
    tables = [cap_table, jam_table, change_coef]
    grids = [density, cap_code, jam_code, adjacency]
    sizes = (12, 4, 4, 3)

    def ends(depth):
        args, specs = [], []
        for x, n in zip(grids, sizes):
            args += [x, x]
            specs += [part(0, n, depth, WIDTH), part(CELLS_HERE // depth - 1, n, depth, WIDTH)]
        return args, specs

    args, specs = ends(8)
    line = [x.reshape(1, WIDTH) for x in (feed_a, feed_b, turn_share, priority)]
    fwd, bwd, record = call(
        pack_kernel, "pack",
        tables + [feed_a, feed_b] + line + [ramp_code.reshape(32, WIDTH)] + args,
        [SCALARS] * 5 + [full(1, WIDTH)] * 4 + [full(32, WIDTH)] + specs,
        [shape(184, WIDTH), shape(184, WIDTH), shape(RECORD, WIDTH)],
        [full(184, WIDTH), full(184, WIDTH), full(RECORD, WIDTH)],
        vmem=60,
    )
    left = lax.ppermute(fwd, "corr", [(i, (i + 1) % ROWS) for i in range(ROWS)])
    right = lax.ppermute(bwd, "corr", [((i + 1) % ROWS, i) for i in range(ROWS)])
    other_end = jnp.where(lax.axis_index("corr") == 0, left[:RECORD], right[:RECORD])
    both = jnp.concatenate([record, other_end], 0)
    both, left, right, density = lax.optimization_barrier((both, left, right, density))
    grids[0] = density
    pieces = [both] + [
        lax.ppermute(both, "lc", [(i, (i + 2 * k) % 8) for i in range(8)]) for k in (1, 2, 3)
    ]
    traffic, acc, low, inner = call(
        inner_kernel, "inner", tables + grids,
        [SCALARS] * 3 + [full(n, CELLS_HERE, WIDTH) for n in sizes],
        [shape(12, CELLS_HERE, WIDTH), shape(16, 8, WIDTH), shape(8, 16, 8, WIDTH), shape(2, 8, WIDTH)],
        [full(12, CELLS_HERE, WIDTH), full(16, 8, WIDTH), full(8, 16, 8, WIDTH), full(2, 8, WIDTH)],
        cells_scratch(16),
        flops=1 << 27,
    )
    pieces = lax.optimization_barrier(tuple(pieces) + (inner,))
    pieces, inner = list(pieces[:-1]), pieces[-1]
    swap = [(i, i ^ 1) for i in range(8)]
    pieces += [lax.ppermute(x, "lc", swap) for x in pieces]
    args, specs = ends(16)
    any_space = pl.BlockSpec(memory_space=pl.ANY)
    traffic, segment, aux, edge_acc, edge_low = call(
        edge_kernel, "edges",
        tables + args + [left, right] + pieces + [inner, traffic],
        [SCALARS] * 3 + specs + [full(184, WIDTH)] * 2 + [full(2 * RECORD, WIDTH)] * 8
        + [full(2, 8, WIDTH), any_space],
        [shape(12, CELLS_HERE, WIDTH), shape(ROWS, 2, 8, WIDTH), shape(4, 8, WIDTH),
         shape(6, 8, WIDTH), shape(8, 6, 8, WIDTH)],
        [any_space, full(ROWS, 2, 8, WIDTH), full(4, 8, WIDTH), full(6, 8, WIDTH),
         full(8, 6, 8, WIDTH)],
        [pltpu.VMEM((23 * 48, WIDTH), F32), pltpu.VMEM((2 * RECORD * 8, WIDTH), F32),
         pltpu.VMEM((STEPS * 12 * 8, WIDTH), F32), pltpu.VMEM((16, WIDTH), F32)]
        + cells_scratch(6)
        + [pltpu.VMEM((2, 12, 8, WIDTH), F32), pltpu.SemaphoreType.DMA((2,))],
        aliases={22: 0},
    )
    segments = lax.all_to_all(segment, "corr", 0, 0)
    queue = call(
        count_kernel, "count", [segments, aux, inner, acc, low, edge_acc, edge_low],
        [full(ROWS, 2, 8, WIDTH), full(4, 8, WIDTH), full(2, 8, WIDTH), full(16, 8, WIDTH),
         full(8, 16, 8, WIDTH), full(6, 8, WIDTH), full(8, 6, 8, WIDTH)],
        shape(CELLS_HERE, WIDTH), full(CELLS_HERE, WIDTH),
        [pltpu.VMEM((3, 8, WIDTH), F32), pltpu.VMEM((3, 8, WIDTH), F32), pltpu.VMEM((48, WIDTH), F32)],
    )
    return traffic.reshape(LANES, CLASSES, CELLS_HERE, WIDTH), queue


def solution(mesh):
    placed = (
        P(None, None, "corr", "lc"),
        P(None, "corr", "lc"),
        P(None, "corr", "lc"),
        P(None, "corr", "lc"),
        P(None, None, "lc"),
        P("lc"),
        P("lc"),
        P("lc"),
        P("lc"),
        P(),
        P(),
        P(),
    )
    return jax.shard_map(
        on_device,
        mesh=mesh,
        in_specs=placed,
        out_specs=(P(None, None, "corr", "lc"), P("corr", "lc")),
        check_vma=False,
    )
```

```python
import jax
import jax.numpy as jnp
from jax import lax
from jax.experimental import pallas as pl
from jax.experimental.pallas import tpu as pltpu
from jax.sharding import PartitionSpec as P

STEPS = 8
LANES = 4
CLASSES = 3
ROWS = 16
WIDTH = 128
CELLS_HERE = 128
BIG = 1e30
F32 = jnp.float32
RAMP_UNIT = 0.01
RAMP_FRACTION = (0.56, 0.16, 0.08)

HEAD_DEPTH = 27
TAIL_DEPTH = 35
RAMP_ROW = 108
FEED_ROW = 140
SHARE_ROW = 141
INVERSE_ROW = 142
RECORD = 152


def inverse(x):
    r = pl.reciprocal(x, approx=True)
    return r * (2.0 - x * r)


def total_of(state):
    return state[0] + 1.5 * state[1] + 2.5 * state[2]


def supply_of(totals, cap, jam, wave):
    return jnp.maximum(jnp.minimum(cap, wave * (jam - totals)), 0.0)


def sent_share(totals, cap, next_supply):
    return jnp.minimum(0.5, jnp.minimum(cap, next_supply) * inverse(totals))


def pick(code, table, count):
    values = [table[i] for i in range(count)]
    bit = 1
    while len(values) > 1:
        on = (code & bit) != 0
        values = [jnp.where(on, values[i + 1], values[i]) for i in range(0, len(values), 2)]
        bit *= 2
    return values[0]


def wave_of(cap, jam):
    return cap / (jam - 2.0 * cap)


def lane_change(state, adjacent, coef):
    moving = [
        [(adjacent[p] * coef[k]) * (state[p][k] - state[p + 1][k]) for k in range(CLASSES)]
        for p in range(LANES - 1)
    ]
    out = []
    for lane in range(LANES):
        row = []
        for k in range(CLASSES):
            value = state[lane][k]
            if lane < LANES - 1:
                value = value - moving[lane][k]
            if lane > 0:
                value = value + moving[lane - 1][k]
            row.append(value)
        out.append(row)
    return out


def middle(a, b, c):
    return jnp.maximum(jnp.minimum(a, b), jnp.minimum(jnp.maximum(a, b), c))


def window(count, refs, step, coef, inject, mask, scan):
    st, tot, cap, jam, wave, adj, level, acc, low = refs
    last = count - 1

    def supply(v):
        return [
            supply_of(tot[lane, v], cap[lane, v], jam[lane, v], wave[lane, v])
            for lane in range(LANES)
        ]

    def flux(v, next_supply):
        out = []
        for lane in range(LANES):
            share = sent_share(tot[lane, v], cap[lane, v], next_supply[lane])
            out.append([st[lane * CLASSES + k, v] * share for k in range(CLASSES)])
        return out

    wrapped = [pltpu.roll(x, 7, 0) for x in supply(0)]
    final = flux(last, wrapped)
    before = [[pltpu.roll(x, 1, 0) for x in row] for row in final]
    running = lowest = None
    for v in range(count):
        leaving = flux(v, supply(v + 1)) if v < last else final
        came, gone = inject(v, before, leaving)
        state = [
            [(st[lane * CLASSES + k, v] + came[lane][k]) - gone[lane][k] for k in range(CLASSES)]
            for lane in range(LANES)
        ]
        state = lane_change(state, [adj[p, v] for p in range(LANES - 1)], coef)
        sums = []
        for lane in range(LANES):
            for k in range(CLASSES):
                st[lane * CLASSES + k, v] = state[lane][k]
            sums.append(total_of(state[lane]))
            tot[lane, v] = sums[lane]
        excess = 0.25 * ((sums[0] + sums[1]) + (sums[2] + sums[3])) - level[v]
        excess = jnp.where(mask(v), excess, 0.0)
        running = excess if running is None else running + excess
        lowest = running if lowest is None else jnp.minimum(lowest, running)
        acc[1, v] = running
        low[step, v] = lowest
        before = leaving
    carry, floor = scan(running, lowest)
    for v in range(count):
        acc[0, v] = acc[0, v] + (carry + acc[1, v])
        low[step, v] = jnp.minimum(floor, carry + low[step, v])


def fill(count, stride, refs, density, cap_code, jam_code, adjacency, cap_table, jam_table):
    st, tot, cap, jam, wave, adj, level, acc = refs
    for v in range(count):
        rows = pl.ds(v, 8, stride=stride)
        around = None
        for lane in range(LANES):
            state = [density(lane * CLASSES + k, rows) for k in range(CLASSES)]
            for k in range(CLASSES):
                st[lane * CLASSES + k, v] = state[k]
            tot[lane, v] = total_of(state)
            c = pick(cap_code(lane, rows), cap_table, 8)
            j = pick(jam_code(lane, rows), jam_table, 4)
            cap[lane, v] = c
            jam[lane, v] = j
            wave[lane, v] = wave_of(c, j)
            around = c if around is None else around + c
        for p in range(LANES - 1):
            adj[p, v] = adjacency(p, rows)
        level[v] = 0.5 * around
        acc[0, v] = jnp.zeros((8, WIDTH), F32)


def pack_kernel(
    cap_table, jam_table, coef_ref, feed_a, feed_b, feed_a_row, feed_b_row, share_row, prio_row,
    ramp, d_lo, d_hi, c_lo, c_hi, j_lo, j_hi, a_lo, a_hi, fwd, bwd, zone,
):
    row_here = lax.axis_index("corr")
    tail = row_here == ROWS - 1
    place = lax.axis_index("lc")
    for out, d, c, j, a in ((bwd, d_lo, c_lo, j_lo, a_lo), (fwd, d_hi, c_hi, j_hi, a_hi)):
        row = 0
        for ref, n in ((d, 12), (c, 4), (j, 4), (a, 3)):
            for i in range(n):
                out[pl.ds(row * 8, 8), :] = ref[i].astype(F32)
                row += 1
    coef = [coef_ref[k] for k in range(CLASSES)]

    def own(lo, hi, i):
        return jnp.where(tail, hi[i], lo[i])

    cap_code = [own(c_lo, c_hi, i) for i in range(LANES)]
    jam_code = [own(j_lo, j_hi, i) for i in range(LANES)]
    near = [own(a_lo, a_hi, i).astype(F32) for i in range(LANES - 1)]
    cap = [pick(x, cap_table, 8) for x in cap_code]
    jam = [pick(x, jam_table, 4) for x in jam_code]
    wave = [wave_of(c, j) for c, j in zip(cap, jam)]
    state = [[own(d_lo, d_hi, lane * CLASSES + k) for k in range(CLASSES)] for lane in range(LANES)]
    history = []
    for d in range(4):
        totals = [total_of(x) for x in state]
        supply = [supply_of(totals[i], cap[i], jam[i], wave[i]) for i in range(LANES)]
        ahead = [pltpu.roll(x, 7, 0) for x in supply]
        out = []
        for i in range(LANES):
            share = sent_share(totals[i], cap[i], ahead[i])
            out.append([x * share for x in state[i]])
        came = [[pltpu.roll(x, 1, 0) for x in row] for row in out]
        history.append((state, ahead, came))
        if d < 3:
            state = [
                [(state[i][k] + came[i][k]) - out[i][k] for k in range(CLASSES)]
                for i in range(LANES)
            ]
            state = lane_change(state, near, coef)
    codes = [x.astype(F32) for x in cap_code + jam_code] + near

    def put(row, value, at):
        zone[pl.ds(row, 1), :] = value[at : at + 1, :]

    @pl.when(tail)
    def _():
        for d in range(4):
            state, _, came = history[d]
            for i in range(LANES):
                for k in range(CLASSES):
                    put(TAIL_DEPTH * d + i * CLASSES + k, state[i][k], 7 - d)
                    put(TAIL_DEPTH * d + 12 + i * CLASSES + k, came[i][k], 7 - d)
            for n, x in enumerate(codes):
                put(TAIL_DEPTH * d + 24 + n, x, 7 - d)
        zone[pl.ds(FEED_ROW, 1), :] = feed_b_row[...].astype(F32)
        zone[pl.ds(SHARE_ROW, 1), :] = share_row[...]

    @pl.when(jnp.logical_not(tail))
    def _():
        for d in range(4):
            state, ahead, _ = history[d]
            for i in range(LANES):
                for k in range(CLASSES):
                    put(HEAD_DEPTH * d + i * CLASSES + k, state[i][k], d)
                put(HEAD_DEPTH * d + 12 + i, ahead[i], d)
            for n, x in enumerate(codes):
                put(HEAD_DEPTH * d + 16 + n, x, d)
        zone[pl.ds(RAMP_ROW, 32), :] = ramp[...].astype(F32)
        zone[pl.ds(FEED_ROW, 1), :] = feed_a_row[...].astype(F32)
        zone[pl.ds(SHARE_ROW, 1), :] = prio_row[...]

    index = lax.broadcasted_iota(jnp.int32, (8, WIDTH), 0) * WIDTH + lax.broadcasted_iota(
        jnp.int32, (8, WIDTH), 1
    )

    def note(c, found):
        feed = jnp.where(tail, feed_b[c], feed_a[c])
        return jnp.where(index == feed, place * WIDTH + c, found)

    found = lax.fori_loop(0, WIDTH, note, jnp.zeros((8, WIDTH), jnp.int32), unroll=16)
    zone[pl.ds(INVERSE_ROW, 8), :] = found.astype(F32)
    zone[pl.ds(INVERSE_ROW + 8, 2), :] = jnp.zeros((2, WIDTH), F32)

    @pl.when(tail)
    def _():
        fwd[pl.ds(0, RECORD), :] = zone[pl.ds(0, RECORD), :]

    @pl.when(row_here == 0)
    def _():
        bwd[pl.ds(0, RECORD), :] = zone[pl.ds(0, RECORD), :]


def inner_kernel(
    cap_table, jam_table, coef_ref, density, cap_code, jam_code, adjacency,
    traffic, acc_out, low, stats, strip, st, tot, cap, jam, wave, adj, level, acc,
):
    coef = [coef_ref[k] for k in range(CLASSES)]
    fill(
        16, 16, (st, tot, cap, jam, wave, adj, level, acc),
        lambda i, rows: density[i, rows, :],
        lambda i, rows: cap_code[i, rows, :],
        lambda i, rows: jam_code[i, rows, :],
        lambda i, rows: adjacency[i, rows, :].astype(F32),
        cap_table, jam_table,
    )
    row = 0
    for ref, n in ((density, 12), (cap_code, 4), (jam_code, 4), (adjacency, 3)):
        for i in range(n):
            strip[pl.ds(row * 32, 16), :] = ref[i, pl.ds(0, 16), :].astype(F32)
            strip[pl.ds(row * 32 + 16, 16), :] = ref[i, pl.ds(CELLS_HERE - 16, 16), :].astype(F32)
            row += 1
    sub = lax.broadcasted_iota(jnp.int32, (8, WIDTH), 0)

    def one(step, carry):
        def scan(running, lowest):
            total, least = running, lowest
            for shift in (1, 2, 4):
                here = sub >= shift
                t = jnp.where(here, pltpu.roll(total, shift, 0), 0.0)
                m = jnp.where(here, pltpu.roll(least, shift, 0), BIG)
                least = jnp.minimum(m, t + least)
                total = t + total
            stats[0, pl.ds(step, 1), :] = total[7:8, :]
            stats[1, pl.ds(step, 1), :] = least[7:8, :]
            return (
                jnp.where(sub >= 1, pltpu.roll(total, 1, 0), 0.0),
                jnp.where(sub >= 1, pltpu.roll(least, 1, 0), BIG),
            )

        window(
            16, (st, tot, cap, jam, wave, adj, level, acc, low), step, coef,
            lambda v, before, leaving: (before, leaving),
            lambda v: (sub != 0) if v < 8 else (sub != 7),
            scan,
        )
        return carry

    lax.fori_loop(0, STEPS, one, 0)
    for v in range(16):
        for i in range(LANES * CLASSES):
            traffic[i, pl.ds(v, 8, stride=16), :] = st[i, v]
        acc_out[v] = acc[0, v]


def whole(x):
    return x.astype(jnp.int32)


def along(x, index, axis):
    dims = lax.GatherDimensionNumbers(
        offset_dims=(), collapsed_slice_dims=(axis,), start_index_map=(axis,),
        operand_batching_dims=(1 - axis,), start_indices_batching_dims=(1 - axis,),
    )
    return lax.gather(
        x, index[:, :, None], dims, (1, 1), mode=lax.GatherScatterMode.PROMISE_IN_BOUNDS
    )


def direct(index):
    chunk = index >> 7
    return index & (WIDTH - 1), [chunk == i for i in range(1, 8)]


def permute_direct(x, how):
    lane, masks = how
    out = None
    for i in range(8):
        got = along(jnp.broadcast_to(x[i : i + 1, :], (8, WIDTH)), lane, 1)
        out = got if out is None else jnp.where(masks[i - 1], got, out)
    return out


TURNS = 4
FACTOR = (1, 1, 1, 3)
RECIPROCAL = (1, 1, 1, 3)


def offset(t, lane):
    low, mid, high = lane & 7, (lane >> 3) & 7, lane >> 6
    return (lane * 0, low, mid, 3 * low + 5 * mid + 4 * high)[t]


def routed(indices, table):
    n = len(indices)
    for p, index in enumerate(indices):
        table[pl.ds(8 * p, 8), :] = index
    used = [jnp.zeros((n, WIDTH), jnp.int32) for _ in range(TURNS)]
    fits = None
    for i in range(8):
        source = table[pl.ds(i, n, stride=8), :]
        row, lane = source >> 7, source & (WIDTH - 1)
        done = None
        key = jnp.zeros((n, WIDTH), jnp.int32)
        for t in range(TURNS):
            slot = (FACTOR[t] * row + offset(t, lane)) & 7
            bit = jnp.left_shift(jnp.ones((n, WIDTH), jnp.int32), slot)
            free = (used[t] & bit) == 0
            take = free if done is None else jnp.logical_and(free, jnp.logical_not(done))
            used[t] = jnp.where(take, used[t] | bit, used[t])
            key = jnp.where(take, 8 * t + slot, key)
            done = take if done is None else jnp.logical_or(done, take)
        fits = done if fits is None else jnp.logical_and(fits, done)
        table[pl.ds(32 + i, n, stride=8), :] = key
    sub = lax.broadcasted_iota(jnp.int32, (8, WIDTH), 0)
    routes = []
    for p, index in enumerate(indices):
        key = table[pl.ds(32 + 8 * p, 8), :]
        lane = index & (WIDTH - 1)
        lanes = [jnp.zeros((8, WIDTH), jnp.int32) for _ in range(TURNS)]
        for i in range(8):
            where = jnp.broadcast_to(key[i : i + 1, :], (8, WIDTH)) - sub
            what = jnp.broadcast_to(lane[i : i + 1, :], (8, WIDTH))
            for t in range(TURNS):
                lanes[t] = jnp.where(where == 8 * t, what, lanes[t])
        turn = key >> 3
        routes.append((lanes, key & 7, [turn == t for t in range(1, TURNS)]))
    return routes, jnp.min(jnp.where(fits, 1.0, 0.0)) > 0.5


def permute_routed(x, how):
    lanes, slot, masks = how
    sub = lax.broadcasted_iota(jnp.int32, (8, WIDTH), 0)
    place = lax.broadcasted_iota(jnp.int32, (8, WIDTH), 1)
    out = None
    for t in range(TURNS):
        y = x if t == 0 else along(x, (RECIPROCAL[t] * (sub - offset(t, place))) & 7, 0)
        got = along(along(y, lanes[t], 1), slot, 0)
        out = got if out is None else jnp.where(masks[t - 1], got, out)
    return out


def junctions(zone, inj, spare_rows, table, cap_table, jam_table, coef):
    def head(row):
        return zone[pl.ds(row * 8, 8), :]

    def tail(row):
        return zone[pl.ds((RECORD + row) * 8, 8), :]

    feed_a = whole(head(FEED_ROW))
    feed_b = whole(tail(FEED_ROW))
    prio = head(SHARE_ROW)
    share = tail(SHARE_ROW)
    for side, read in enumerate((head, tail)):
        for i in range(8):
            spare_rows[pl.ds(side * 8 + i, 1), :] = jnp.sum(
                read(INVERSE_ROW + i), axis=0, keepdims=True
            )
    back_from_a = whole(spare_rows[pl.ds(0, 8), :])
    back_from_b = whole(spare_rows[pl.ds(8, 8), :])

    indices = (feed_a, feed_b, back_from_a, back_from_b)
    routes, fits = routed(indices, table)
    fixed = (head, tail, prio, share, inj, cap_table, jam_table, coef)

    @pl.when(fits)
    def _():
        simulate(fixed, routes, permute_routed)

    @pl.when(jnp.logical_not(fits))
    def _():
        simulate(fixed, [direct(x) for x in indices], permute_direct)


def simulate(fixed, routes, permute):
    head, tail, prio, share, inj, cap_table, jam_table, coef = fixed
    head_row = lax.axis_index("corr") == 0
    plan_a, plan_b, plan_ra, plan_rb = routes

    def statics(read, base):
        cap = [pick(whole(read(base + i)), cap_table, 8) for i in range(LANES)]
        jam = [pick(whole(read(base + 4 + i)), jam_table, 4) for i in range(LANES)]
        wave = [wave_of(c, j) for c, j in zip(cap, jam)]
        return cap, jam, wave, [read(base + 8 + p) for p in range(LANES - 1)]

    head_fixed = [statics(head, HEAD_DEPTH * d + 16) for d in range(4)]
    tail_fixed = [statics(tail, TAIL_DEPTH * d + 24) for d in range(4)]

    def first(read, base):
        return [[read(base + i * CLASSES + k) for k in range(CLASSES)] for i in range(LANES)]

    def supplies(state, fixed):
        return [
            supply_of(total_of(state[i]), fixed[0][i], fixed[1][i], fixed[2][i])
            for i in range(LANES)
        ]

    def fluxes(state, fixed, next_supply):
        out = []
        for i in range(LANES):
            q = sent_share(total_of(state[i]), fixed[0][i], next_supply[i])
            out.append([x * q for x in state[i]])
        return out

    heads, tails = {}, {}
    for step in range(STEPS):
        if step < 4:
            heads[step] = first(head, HEAD_DEPTH * step)
            tails[step] = first(tail, TAIL_DEPTH * step)
        deep = min(step, 6 - step)
        supply = supplies(heads[0], head_fixed[0])
        arriving, rates = [], []
        for i in range(LANES):
            state = tails[0][i]
            speed = jnp.minimum(0.5, tail_fixed[0][0][i] * inverse(total_of(state)))
            demand = [x * speed for x in state]
            part_a = [share * x for x in demand]
            part_b = [x - y for x, y in zip(demand, part_a)]
            take_a = [permute(x, plan_a) for x in part_a]
            take_b = [permute(x, plan_b) for x in part_b]
            need_a = total_of(take_a)
            need_b = total_of(take_b)
            s = supply[i]
            share_a = prio * s
            share_b = (1.0 - prio) * s
            pass_a = jnp.minimum(need_a, middle(need_a, s - need_b, share_a))
            pass_b = jnp.minimum(need_b, middle(need_b, s - need_a, share_b))
            rate_a = pass_a / need_a
            rate_b = pass_b / need_b
            ramp = jnp.minimum(
                head(RAMP_ROW + step * LANES + i) * RAMP_UNIT,
                jnp.maximum((s - pass_a) - pass_b, 0.0),
            )
            arriving.append(
                [
                    (take_a[k] * rate_a + take_b[k] * rate_b) + RAMP_FRACTION[k] * ramp
                    for k in range(CLASSES)
                ]
            )
            back_a = permute(rate_a, plan_ra)
            back_b = permute(rate_b, plan_rb)
            rates.append([part_a[k] * back_a + part_b[k] * back_b for k in range(CLASSES)])
        for i in range(LANES):
            for k in range(CLASSES):
                inj[pl.ds((step * 12 + i * CLASSES + k) * 8, 8), :] = jnp.where(
                    head_row, arriving[i][k], rates[i][k]
                )
        if step == STEPS - 1:
            break
        new_heads, new_tails = {}, {}
        came, gone = arriving, rates
        for d in range(deep + 1):
            if d < deep or deep < step:
                ahead = supplies(heads[d + 1], head_fixed[d + 1])
                entering = fluxes(tails[d + 1], tail_fixed[d + 1], supplies(tails[d], tail_fixed[d]))
            else:
                ahead = [head(HEAD_DEPTH * d + 12 + i) for i in range(LANES)]
                entering = first(tail, TAIL_DEPTH * d + 12)
            out = fluxes(heads[d], head_fixed[d], ahead)
            moved = [
                [(heads[d][i][k] + came[i][k]) - out[i][k] for k in range(CLASSES)]
                for i in range(LANES)
            ]
            new_heads[d] = lane_change(moved, head_fixed[d][3], coef)
            moved = [
                [(tails[d][i][k] + entering[i][k]) - gone[i][k] for k in range(CLASSES)]
                for i in range(LANES)
            ]
            new_tails[d] = lane_change(moved, tail_fixed[d][3], coef)
            came, gone = out, entering
        heads, tails = new_heads, new_tails


def edge_kernel(
    cap_table, jam_table, coef_ref, strip, left, right,
    e0, e1, e2, e3, e4, e5, e6, e7, inner, rim, segment, aux, acc_out, low,
    nat, zone, inj, spare_rows, table, st, tot, cap, jam, wave, adj, level, acc,
):
    row = lax.axis_index("corr")
    place = lax.axis_index("lc")
    coef = [coef_ref[k] for k in range(CLASSES)]
    first_row = row == 0
    last_row = row == ROWS - 1

    @pl.when(jnp.logical_or(first_row, last_row))
    def _():
        for n, ends in enumerate((e0, e1, e2, e3, e4, e5, e6, e7)):
            chip = (place // 2 + (4 - n % 4)) % 4
            core = place % 2 if n < 4 else 1 - place % 2
            for m in range(2):
                side = jnp.where(first_row, m, 1 - m)
                base = side * (RECORD * 8) + 2 * chip + core
                for r in range(RECORD // 8):
                    zone[pl.ds(base + r * 64, 8, stride=8), :] = ends[
                        pl.ds(m * RECORD + r * 8, 8), :
                    ]
        junctions(zone, inj, spare_rows, table, cap_table, jam_table, coef)

    for i in range(23):
        nat[pl.ds(i * 48, 8), :] = left[pl.ds(i * 8, 8), :]
        nat[pl.ds(i * 48 + 8, 32), :] = strip[pl.ds(i * 32, 32), :]
        nat[pl.ds(i * 48 + 40, 8), :] = right[pl.ds(i * 8, 8), :]

    def rows_of(base):
        def read(i, rows):
            return nat[pl.ds((base + i) * 48 + rows.start, 8, stride=6), :]

        return read

    def code_of(base):
        read = rows_of(base)
        return lambda i, rows: read(i, rows).astype(jnp.int32)

    fill(
        6, 6, (st, tot, cap, jam, wave, adj, level, acc),
        rows_of(0), code_of(12), code_of(16), rows_of(20), cap_table, jam_table,
    )
    sub = lax.broadcasted_iota(jnp.int32, (8, WIDTH), 0)
    in_strip = sub % 4
    at_head = jnp.logical_and(sub == 1, first_row)
    at_tail = jnp.logical_and(sub == 6, last_row)

    def one(step, carry):
        def injected(i, k):
            return jnp.broadcast_to(
                inj[pl.ds((step * 12 + i * CLASSES + k) * 8 + place, 1), :], (8, WIDTH)
            )

        def inject(v, before, leaving):
            came, gone = before, leaving
            if v == 2:
                came = [
                    [jnp.where(at_head, injected(i, k), before[i][k]) for k in range(CLASSES)]
                    for i in range(LANES)
                ]
            if v == 3:
                gone = [
                    [jnp.where(at_tail, injected(i, k), leaving[i][k]) for k in range(CLASSES)]
                    for i in range(LANES)
                ]
            return came, gone

        def mask(v):
            if v < 2:
                return in_strip == 2
            if v < 4:
                return jnp.logical_or(in_strip == 1, in_strip == 2)
            return in_strip == 1

        def scan(running, lowest):
            second = in_strip == 2
            carry = jnp.where(second, pltpu.roll(running, 1, 0), 0.0)
            floor = jnp.where(second, pltpu.roll(lowest, 1, 0), BIG)
            total = carry + running
            least = jnp.minimum(floor, carry + lowest)
            aux[0, pl.ds(step, 1), :] = total[2:3, :]
            aux[1, pl.ds(step, 1), :] = least[2:3, :]
            aux[2, pl.ds(step, 1), :] = total[6:7, :]
            aux[3, pl.ds(step, 1), :] = least[6:7, :]
            return carry, floor

        window(
            6, (st, tot, cap, jam, wave, adj, level, acc, low), step, coef, inject, mask, scan
        )
        return carry

    lax.fori_loop(0, STEPS, one, 0)
    for v in range(6):
        for i in range(LANES * CLASSES):
            nat[pl.ds(i * 48 + v, 8, stride=6), :] = st[i, v]
        acc_out[v] = acc[0, v]
    for i in range(LANES * CLASSES):
        rim[0, i] = nat[pl.ds(i * 48 + 8, 8), :]
        rim[1, i] = nat[pl.ds(i * 48 + 32, 8), :]
    left_sum, left_low = aux[0], aux[1]
    most_sum = left_sum + inner[0]
    most_low = jnp.minimum(left_low, left_sum + inner[1])
    all_sum = most_sum + aux[2]
    all_low = jnp.minimum(most_low, most_sum + aux[3])
    for i in range(ROWS):
        segment[i, 0] = all_sum
        segment[i, 1] = all_low


def count_kernel(
    segments, aux, inner, acc, low, edge_acc, edge_low, rim, traffic_in,
    queue, traffic, sums, floors, nat, sem,
):
    del traffic_in
    copies = [
        pltpu.make_async_copy(rim.at[0], traffic.at[:, pl.ds(0, 8), :], sem.at[0]),
        pltpu.make_async_copy(rim.at[1], traffic.at[:, pl.ds(CELLS_HERE - 8, 8), :], sem.at[1]),
    ]
    for copy in copies:
        copy.start()
    row = lax.axis_index("corr")
    total = jnp.zeros((8, WIDTH), F32)
    least = jnp.zeros((8, WIDTH), F32)
    for i in range(ROWS - 1):
        on = i < row
        least = jnp.where(on, jnp.minimum(least, total + segments[i, 1]), least)
        total = jnp.where(on, total + segments[i, 0], total)
    mid_total = total + aux[0]
    mid_least = jnp.minimum(least, total + aux[1])
    end_total = mid_total + inner[0]
    end_least = jnp.minimum(mid_least, mid_total + inner[1])
    for n, (t, m) in enumerate(((total, least), (mid_total, mid_least), (end_total, end_least))):
        sums[n] = t
        floors[n] = m
    scale = 1.0 / (STEPS * CELLS_HERE * ROWS)
    left = lax.broadcasted_iota(jnp.int32, (8, WIDTH), 0) < 4

    def spread(ref, n, step):
        return jnp.broadcast_to(ref[n, pl.ds(step, 1), :], (8, WIDTH))

    inside = [(spread(sums, 1, s), spread(floors, 1, s)) for s in range(STEPS)]
    for v in range(16):
        value = acc[v]
        for s in range(STEPS):
            value = value + (inside[s][0] - jnp.minimum(inside[s][1], inside[s][0] + low[s, v]))
        queue[pl.ds(v, 8, stride=16), :] = value * scale
    edges = [
        (
            jnp.where(left, spread(sums, 0, s), spread(sums, 2, s)),
            jnp.where(left, spread(floors, 0, s), spread(floors, 2, s)),
        )
        for s in range(STEPS)
    ]
    for v in range(6):
        value = edge_acc[v]
        for s in range(STEPS):
            value = value + (edges[s][0] - jnp.minimum(edges[s][1], edges[s][0] + edge_low[s, v]))
        nat[pl.ds(v, 8, stride=6), :] = value * scale
    queue[pl.ds(0, 8), :] = nat[pl.ds(8, 8), :]
    queue[pl.ds(CELLS_HERE - 8, 8), :] = nat[pl.ds(32, 8), :]
    for copy in copies:
        copy.wait()


def shape(*dims):
    return jax.ShapeDtypeStruct(dims, F32)


def full(*dims):
    return pl.BlockSpec(dims, lambda i: (0,) * len(dims))


def part(place, *dims):
    return pl.BlockSpec(dims, lambda i: (0, place, 0))


SCALARS = pl.BlockSpec(memory_space=pltpu.SMEM)
HERE = pl.BlockSpec(memory_space=pltpu.VMEM)


def call(kernel, name, args, in_specs, outs, out_specs, scratch=(), aliases=None, flops=0, vmem=32, grid=(1,)):
    return pl.pallas_call(
        kernel,
        grid=grid,
        in_specs=in_specs,
        out_specs=out_specs,
        out_shape=outs,
        scratch_shapes=scratch,
        input_output_aliases=aliases or {},
        compiler_params=pltpu.CompilerParams(vmem_limit_bytes=vmem << 20),
        cost_estimate=pl.CostEstimate(flops=flops, bytes_accessed=4 << 20, transcendentals=0),
        name=name,
    )(*args)


def cells_scratch(count):
    def hold(n):
        return pltpu.VMEM((n, count, 8, WIDTH), F32)

    return [hold(12), hold(4), hold(4), hold(4), hold(4), hold(3), pltpu.VMEM((count, 8, WIDTH), F32), hold(2)]


def on_device(
    density, cap_code, jam_code, adjacency, ramp_code, feed_a, feed_b, turn_share, priority,
    cap_table, jam_table, change_coef,
):
    density = density.reshape(12, CELLS_HERE, WIDTH)
    tables = [cap_table, jam_table, change_coef]
    grids = [density, cap_code, jam_code, adjacency]
    sizes = (12, 4, 4, 3)

    def ends(depth):
        args, specs = [], []
        for x, n in zip(grids, sizes):
            args += [x, x]
            specs += [part(0, n, depth, WIDTH), part(CELLS_HERE // depth - 1, n, depth, WIDTH)]
        return args, specs

    args, specs = ends(8)
    line = [x.reshape(1, WIDTH) for x in (feed_a, feed_b, turn_share, priority)]
    fwd, bwd, both = call(
        pack_kernel, "pack",
        tables + [feed_a, feed_b] + line + [ramp_code.reshape(32, WIDTH)] + args,
        [SCALARS] * 5 + [full(1, WIDTH)] * 4 + [full(32, WIDTH)] + specs,
        [shape(184, WIDTH), shape(184, WIDTH), shape(2 * RECORD, WIDTH)],
        [full(184, WIDTH), full(184, WIDTH), full(2 * RECORD, WIDTH)],
        vmem=60,
    )
    left = lax.ppermute(fwd, "corr", [(i, (i + 1) % ROWS) for i in range(ROWS)])
    right = lax.ppermute(bwd, "corr", [((i + 1) % ROWS, i) for i in range(ROWS)])
    other_end = jnp.where(lax.axis_index("corr") == 0, left[:RECORD], right[:RECORD])
    both = lax.dynamic_update_slice(both, other_end, (RECORD, 0))
    both, left, right, density = lax.optimization_barrier((both, left, right, density))
    grids[0] = density
    pieces = [both] + [
        lax.ppermute(both, "lc", [(i, (i + 2 * k) % 8) for i in range(8)]) for k in (1, 2, 3)
    ]
    traffic, acc, low, inner, strip = call(
        inner_kernel, "inner", tables + grids,
        [SCALARS] * 3 + [full(n, CELLS_HERE, WIDTH) for n in sizes],
        [shape(12, CELLS_HERE, WIDTH), shape(16, 8, WIDTH), shape(8, 16, 8, WIDTH), shape(2, 8, WIDTH),
         shape(23 * 32, WIDTH)],
        [full(12, CELLS_HERE, WIDTH), full(16, 8, WIDTH), full(8, 16, 8, WIDTH), full(2, 8, WIDTH),
         full(23 * 32, WIDTH)],
        cells_scratch(16),
        flops=1 << 27,
    )
    swap = [(i, i ^ 1) for i in range(8)]
    swapped = [lax.ppermute(both, "lc", swap)]
    for n in (1, 2, 3):
        pieces[n], inner = lax.optimization_barrier((pieces[n], inner))
        swapped.append(lax.ppermute(pieces[n], "lc", swap))
    pieces = pieces + swapped
    any_space = pl.BlockSpec(memory_space=pl.ANY)
    rim, segment, aux, edge_acc, edge_low = call(
        edge_kernel, "edges",
        tables + [strip, left, right] + pieces + [inner],
        [SCALARS] * 3 + [HERE] * 12,
        [shape(2, 12, 8, WIDTH), shape(ROWS, 2, 8, WIDTH), shape(4, 8, WIDTH),
         shape(6, 8, WIDTH), shape(8, 6, 8, WIDTH)],
        [HERE] * 5,
        [pltpu.VMEM((23 * 48, WIDTH), F32), pltpu.VMEM((2 * RECORD * 8, WIDTH), F32),
         pltpu.VMEM((STEPS * 12 * 8, WIDTH), F32), pltpu.VMEM((16, WIDTH), F32),
         pltpu.VMEM((64, WIDTH), jnp.int32)]
        + cells_scratch(6),
        grid=(),
    )
    segments = lax.all_to_all(segment, "corr", 0, 0)
    queue, traffic = call(
        count_kernel, "count",
        [segments, aux, inner, acc, low, edge_acc, edge_low, rim, traffic],
        [HERE] * 8 + [any_space],
        [shape(CELLS_HERE, WIDTH), shape(12, CELLS_HERE, WIDTH)], [HERE, any_space],
        [pltpu.VMEM((3, 8, WIDTH), F32), pltpu.VMEM((3, 8, WIDTH), F32), pltpu.VMEM((48, WIDTH), F32),
         pltpu.SemaphoreType.DMA((2,))],
        aliases={8: 1}, grid=(),
    )
    return traffic.reshape(LANES, CLASSES, CELLS_HERE, WIDTH), queue


def solution(mesh):
    placed = (
        P(None, None, "corr", "lc"),
        P(None, "corr", "lc"),
        P(None, "corr", "lc"),
        P(None, "corr", "lc"),
        P(None, None, "lc"),
        P("lc"),
        P("lc"),
        P("lc"),
        P("lc"),
        P(),
        P(),
        P(),
    )
    return jax.shard_map(
        on_device,
        mesh=mesh,
        in_specs=placed,
        out_specs=(P(None, None, "corr", "lc"), P("corr", "lc")),
        check_vma=False,
    )
```

```python
import jax
import jax.numpy as jnp
from jax import lax
from jax.experimental import pallas as pl
from jax.experimental.pallas import tpu as pltpu
from jax.sharding import PartitionSpec as P

STEPS = 8
HALF = 4
LANES = 4
CLASSES = 3
ROWS = 16
WIDTH = 128
CELLS_HERE = 128
BIG = 1e30
F32 = jnp.float32
RAMP_UNIT = 0.01
RAMP_FRACTION = (0.56, 0.16, 0.08)

HEAD_DEPTH = 27
TAIL_DEPTH = 35
RAMP_ROW = 108
FEED_ROW = 140
SHARE_ROW = 141
INVERSE_ROW = 142
RECORD = 152


def inverse(x):
    r = pl.reciprocal(x, approx=True)
    return r * (2.0 - x * r)


def total_of(state):
    return state[0] + 1.5 * state[1] + 2.5 * state[2]


def supply_of(totals, cap, jam, wave):
    return jnp.maximum(jnp.minimum(cap, wave * (jam - totals)), 0.0)


def sent_share(totals, cap, next_supply):
    return jnp.minimum(0.5, jnp.minimum(cap, next_supply) * inverse(totals))


def pick(code, table, count):
    values = [table[i] for i in range(count)]
    bit = 1
    while len(values) > 1:
        on = (code & bit) != 0
        values = [jnp.where(on, values[i + 1], values[i]) for i in range(0, len(values), 2)]
        bit *= 2
    return values[0]


def wave_of(cap, jam):
    return cap / (jam - 2.0 * cap)


def lane_change(state, adjacent, coef):
    moving = [
        [(adjacent[p] * coef[k]) * (state[p][k] - state[p + 1][k]) for k in range(CLASSES)]
        for p in range(LANES - 1)
    ]
    out = []
    for lane in range(LANES):
        row = []
        for k in range(CLASSES):
            value = state[lane][k]
            if lane < LANES - 1:
                value = value - moving[lane][k]
            if lane > 0:
                value = value + moving[lane - 1][k]
            row.append(value)
        out.append(row)
    return out


def middle(a, b, c):
    return jnp.maximum(jnp.minimum(a, b), jnp.minimum(jnp.maximum(a, b), c))


def window(count, refs, step, coef, inject, mask, scan):
    st, tot, cap, jam, wave, adj, level, acc, low = refs
    last = count - 1

    def supply(v):
        return [
            supply_of(tot[lane, v], cap[lane, v], jam[lane, v], wave[lane, v])
            for lane in range(LANES)
        ]

    def flux(v, next_supply):
        out = []
        for lane in range(LANES):
            share = sent_share(tot[lane, v], cap[lane, v], next_supply[lane])
            out.append([st[lane * CLASSES + k, v] * share for k in range(CLASSES)])
        return out

    wrapped = [pltpu.roll(x, 7, 0) for x in supply(0)]
    final = flux(last, wrapped)
    before = [[pltpu.roll(x, 1, 0) for x in row] for row in final]
    running = lowest = None
    for v in range(count):
        leaving = flux(v, supply(v + 1)) if v < last else final
        came, gone = inject(v, before, leaving)
        state = [
            [(st[lane * CLASSES + k, v] + came[lane][k]) - gone[lane][k] for k in range(CLASSES)]
            for lane in range(LANES)
        ]
        state = lane_change(state, [adj[p, v] for p in range(LANES - 1)], coef)
        sums = []
        for lane in range(LANES):
            for k in range(CLASSES):
                st[lane * CLASSES + k, v] = state[lane][k]
            sums.append(total_of(state[lane]))
            tot[lane, v] = sums[lane]
        excess = 0.25 * ((sums[0] + sums[1]) + (sums[2] + sums[3])) - level[v]
        excess = jnp.where(mask(v), excess, 0.0)
        running = excess if running is None else running + excess
        lowest = running if lowest is None else jnp.minimum(lowest, running)
        acc[1, v] = running
        low[step, v] = lowest
        before = leaving
    carry, floor = scan(running, lowest)
    for v in range(count):
        acc[0, v] = acc[0, v] + (carry + acc[1, v])
        low[step, v] = jnp.minimum(floor, carry + low[step, v])


def fill(count, stride, refs, density, cap_code, jam_code, adjacency, cap_table, jam_table):
    st, tot, cap, jam, wave, adj, level, acc = refs
    def one(v, carry):
        rows = pl.ds(v, 8, stride=stride)
        around = None
        for lane in range(LANES):
            state = [density(lane * CLASSES + k, rows) for k in range(CLASSES)]
            for k in range(CLASSES):
                st[lane * CLASSES + k, v] = state[k]
            tot[lane, v] = total_of(state)
            c = pick(cap_code(lane, rows), cap_table, 8)
            j = pick(jam_code(lane, rows), jam_table, 4)
            cap[lane, v] = c
            jam[lane, v] = j
            wave[lane, v] = wave_of(c, j)
            around = c if around is None else around + c
        for p in range(LANES - 1):
            adj[p, v] = adjacency(p, rows)
        level[v] = 0.5 * around
        acc[0, v] = jnp.zeros((8, WIDTH), F32)
        return carry

    lax.fori_loop(0, count, one, 0)


def pack_kernel(
    cap_table, jam_table, coef_ref, feed_a, feed_b, feed_a_row, feed_b_row, share_row, prio_row,
    ramp, d_lo, d_hi, c_lo, c_hi, j_lo, j_hi, a_lo, a_hi, fwd, bwd, zone,
):
    row_here = lax.axis_index("corr")
    tail = row_here == ROWS - 1
    place = lax.axis_index("lc")
    for out, d, c, j, a in ((bwd, d_lo, c_lo, j_lo, a_lo), (fwd, d_hi, c_hi, j_hi, a_hi)):
        row = 0
        for ref, n in ((d, 12), (c, 4), (j, 4), (a, 3)):
            for i in range(n):
                out[pl.ds(row * 8, 8), :] = ref[i].astype(F32)
                row += 1
    coef = [coef_ref[k] for k in range(CLASSES)]

    def own(lo, hi, i):
        return jnp.where(tail, hi[i], lo[i])

    cap_code = [own(c_lo, c_hi, i) for i in range(LANES)]
    jam_code = [own(j_lo, j_hi, i) for i in range(LANES)]
    near = [own(a_lo, a_hi, i).astype(F32) for i in range(LANES - 1)]
    cap = [pick(x, cap_table, 8) for x in cap_code]
    jam = [pick(x, jam_table, 4) for x in jam_code]
    wave = [wave_of(c, j) for c, j in zip(cap, jam)]
    state = [[own(d_lo, d_hi, lane * CLASSES + k) for k in range(CLASSES)] for lane in range(LANES)]
    history = []
    for d in range(4):
        totals = [total_of(x) for x in state]
        supply = [supply_of(totals[i], cap[i], jam[i], wave[i]) for i in range(LANES)]
        ahead = [pltpu.roll(x, 7, 0) for x in supply]
        out = []
        for i in range(LANES):
            share = sent_share(totals[i], cap[i], ahead[i])
            out.append([x * share for x in state[i]])
        came = [[pltpu.roll(x, 1, 0) for x in row] for row in out]
        history.append((state, ahead, came))
        if d < 3:
            state = [
                [(state[i][k] + came[i][k]) - out[i][k] for k in range(CLASSES)]
                for i in range(LANES)
            ]
            state = lane_change(state, near, coef)
    codes = [x.astype(F32) for x in cap_code + jam_code] + near

    def put(row, value, at):
        zone[pl.ds(row, 1), :] = value[at : at + 1, :]

    @pl.when(tail)
    def _():
        for d in range(4):
            state, _, came = history[d]
            for i in range(LANES):
                for k in range(CLASSES):
                    put(TAIL_DEPTH * d + i * CLASSES + k, state[i][k], 7 - d)
                    put(TAIL_DEPTH * d + 12 + i * CLASSES + k, came[i][k], 7 - d)
            for n, x in enumerate(codes):
                put(TAIL_DEPTH * d + 24 + n, x, 7 - d)
        zone[pl.ds(FEED_ROW, 1), :] = feed_b_row[...].astype(F32)
        zone[pl.ds(SHARE_ROW, 1), :] = share_row[...]

    @pl.when(jnp.logical_not(tail))
    def _():
        for d in range(4):
            state, ahead, _ = history[d]
            for i in range(LANES):
                for k in range(CLASSES):
                    put(HEAD_DEPTH * d + i * CLASSES + k, state[i][k], d)
                put(HEAD_DEPTH * d + 12 + i, ahead[i], d)
            for n, x in enumerate(codes):
                put(HEAD_DEPTH * d + 16 + n, x, d)
        zone[pl.ds(RAMP_ROW, 32), :] = ramp[...].astype(F32)
        zone[pl.ds(FEED_ROW, 1), :] = feed_a_row[...].astype(F32)
        zone[pl.ds(SHARE_ROW, 1), :] = prio_row[...]

    index = lax.broadcasted_iota(jnp.int32, (8, WIDTH), 0) * WIDTH + lax.broadcasted_iota(
        jnp.int32, (8, WIDTH), 1
    )

    def note(c, found):
        feed = jnp.where(tail, feed_b[c], feed_a[c])
        return jnp.where(index == feed, place * WIDTH + c, found)

    found = lax.fori_loop(0, WIDTH, note, jnp.zeros((8, WIDTH), jnp.int32), unroll=16)
    zone[pl.ds(INVERSE_ROW, 8), :] = found.astype(F32)
    zone[pl.ds(INVERSE_ROW + 8, 2), :] = jnp.zeros((2, WIDTH), F32)

    @pl.when(tail)
    def _():
        fwd[pl.ds(0, RECORD), :] = zone[pl.ds(0, RECORD), :]

    @pl.when(row_here == 0)
    def _():
        bwd[pl.ds(0, RECORD), :] = zone[pl.ds(0, RECORD), :]


def inner_steps(begin, end, coef, refs, stats):
    sub = lax.broadcasted_iota(jnp.int32, (8, WIDTH), 0)

    def one(step, carry):
        def scan(running, lowest):
            total, least = running, lowest
            for shift in (1, 2, 4):
                here = sub >= shift
                t = jnp.where(here, pltpu.roll(total, shift, 0), 0.0)
                m = jnp.where(here, pltpu.roll(least, shift, 0), BIG)
                least = jnp.minimum(m, t + least)
                total = t + total
            stats[0, pl.ds(step, 1), :] = total[7:8, :]
            stats[1, pl.ds(step, 1), :] = least[7:8, :]
            return (
                jnp.where(sub >= 1, pltpu.roll(total, 1, 0), 0.0),
                jnp.where(sub >= 1, pltpu.roll(least, 1, 0), BIG),
            )

        window(
            16, refs, step, coef,
            lambda v, before, leaving: (before, leaving),
            lambda v: (sub != 0) if v < 8 else (sub != 7),
            scan,
        )
        return carry

    lax.fori_loop(begin, end, one, 0)


def early_kernel(
    cap_table, jam_table, coef_ref, density, cap_code, jam_code, adjacency,
    low, stats, strip, st, tot, cap, jam, wave, adj, level, acc,
):
    coef = [coef_ref[k] for k in range(CLASSES)]
    fill(
        16, 16, (st, tot, cap, jam, wave, adj, level, acc),
        lambda i, rows: density[i, rows, :],
        lambda i, rows: cap_code[i, rows, :],
        lambda i, rows: jam_code[i, rows, :],
        lambda i, rows: adjacency[i, rows, :].astype(F32),
        cap_table, jam_table,
    )
    row = 0
    for ref, n in ((density, 12), (cap_code, 4), (jam_code, 4), (adjacency, 3)):
        for i in range(n):
            strip[pl.ds(row * 32, 16), :] = ref[i, pl.ds(0, 16), :].astype(F32)
            strip[pl.ds(row * 32 + 16, 16), :] = ref[i, pl.ds(CELLS_HERE - 16, 16), :].astype(F32)
            row += 1
    inner_steps(
        0, HALF, coef, (st, tot, cap, jam, wave, adj, level, acc, low), stats
    )


def late_kernel(
    coef_ref, early_stats, st_in, tot_in, cap, jam, wave, adj, level, acc_in,
    traffic, acc_out, low, stats, st, tot, acc,
):
    coef = [coef_ref[k] for k in range(CLASSES)]
    stats[...] = early_stats[...]
    for v in range(16):
        for i in range(LANES * CLASSES):
            st[i, v] = st_in[i, v]
        for i in range(LANES):
            tot[i, v] = tot_in[i, v]
        acc[0, v] = acc_in[0, v]
    inner_steps(
        HALF, STEPS, coef, (st, tot, cap, jam, wave, adj, level, acc, low), stats
    )
    for v in range(16):
        for i in range(LANES * CLASSES):
            traffic[i, pl.ds(v, 8, stride=16), :] = st[i, v]
        acc_out[v] = acc[0, v]


def whole(x):
    return x.astype(jnp.int32)


def along(x, index, axis):
    dims = lax.GatherDimensionNumbers(
        offset_dims=(), collapsed_slice_dims=(axis,), start_index_map=(axis,),
        operand_batching_dims=(1 - axis,), start_indices_batching_dims=(1 - axis,),
    )
    return lax.gather(
        x, index[:, :, None], dims, (1, 1), mode=lax.GatherScatterMode.PROMISE_IN_BOUNDS
    )


def direct(index):
    chunk = index >> 7
    return index & (WIDTH - 1), [chunk == i for i in range(1, 8)]


def permute_direct(x, how):
    lane, masks = how
    out = None
    for i in range(8):
        got = along(jnp.broadcast_to(x[i : i + 1, :], (8, WIDTH)), lane, 1)
        out = got if out is None else jnp.where(masks[i - 1], got, out)
    return out


TURNS = 4
FACTOR = (1, 1, 1, 3)
RECIPROCAL = (1, 1, 1, 3)


def offset(t, lane):
    low, mid, high = lane & 7, (lane >> 3) & 7, lane >> 6
    return (lane * 0, low, mid, 3 * low + 5 * mid + 4 * high)[t]


def routed(indices, table):
    n = len(indices)
    for p, index in enumerate(indices):
        table[pl.ds(8 * p, 8), :] = index
    used = [jnp.zeros((n, WIDTH), jnp.int32) for _ in range(TURNS)]
    fits = None
    for i in range(8):
        source = table[pl.ds(i, n, stride=8), :]
        row, lane = source >> 7, source & (WIDTH - 1)
        done = None
        key = jnp.zeros((n, WIDTH), jnp.int32)
        for t in range(TURNS):
            slot = (FACTOR[t] * row + offset(t, lane)) & 7
            bit = jnp.left_shift(jnp.ones((n, WIDTH), jnp.int32), slot)
            free = (used[t] & bit) == 0
            take = free if done is None else jnp.logical_and(free, jnp.logical_not(done))
            used[t] = jnp.where(take, used[t] | bit, used[t])
            key = jnp.where(take, 8 * t + slot, key)
            done = take if done is None else jnp.logical_or(done, take)
        fits = done if fits is None else jnp.logical_and(fits, done)
        table[pl.ds(32 + i, n, stride=8), :] = key
    sub = lax.broadcasted_iota(jnp.int32, (8, WIDTH), 0)
    routes = []
    for p, index in enumerate(indices):
        key = table[pl.ds(32 + 8 * p, 8), :]
        lane = index & (WIDTH - 1)
        lanes = [jnp.zeros((8, WIDTH), jnp.int32) for _ in range(TURNS)]
        for i in range(8):
            where = jnp.broadcast_to(key[i : i + 1, :], (8, WIDTH)) - sub
            what = jnp.broadcast_to(lane[i : i + 1, :], (8, WIDTH))
            for t in range(TURNS):
                lanes[t] = jnp.where(where == 8 * t, what, lanes[t])
        turn = key >> 3
        routes.append((lanes, key & 7, [turn == t for t in range(1, TURNS)]))
    return routes, jnp.min(jnp.where(fits, 1.0, 0.0)) > 0.5


def permute_routed(x, how):
    lanes, slot, masks = how
    sub = lax.broadcasted_iota(jnp.int32, (8, WIDTH), 0)
    place = lax.broadcasted_iota(jnp.int32, (8, WIDTH), 1)
    out = None
    for t in range(TURNS):
        y = x if t == 0 else along(x, (RECIPROCAL[t] * (sub - offset(t, place))) & 7, 0)
        got = along(along(y, lanes[t], 1), slot, 0)
        out = got if out is None else jnp.where(masks[t - 1], got, out)
    return out


def junctions(zone, inj, spare_rows, table, cap_table, jam_table, coef):
    def head(row):
        return zone[pl.ds(row * 8, 8), :]

    def tail(row):
        return zone[pl.ds((RECORD + row) * 8, 8), :]

    feed_a = whole(head(FEED_ROW))
    feed_b = whole(tail(FEED_ROW))
    prio = head(SHARE_ROW)
    share = tail(SHARE_ROW)
    for side, read in enumerate((head, tail)):
        for i in range(8):
            spare_rows[pl.ds(side * 8 + i, 1), :] = jnp.sum(
                read(INVERSE_ROW + i), axis=0, keepdims=True
            )
    back_from_a = whole(spare_rows[pl.ds(0, 8), :])
    back_from_b = whole(spare_rows[pl.ds(8, 8), :])

    indices = (feed_a, feed_b, back_from_a, back_from_b)
    routes, fits = routed(indices, table)
    fixed = (head, tail, prio, share, inj, cap_table, jam_table, coef)

    @pl.when(fits)
    def _():
        simulate(fixed, routes, permute_routed)

    @pl.when(jnp.logical_not(fits))
    def _():
        simulate(fixed, [direct(x) for x in indices], permute_direct)


def simulate(fixed, routes, permute):
    head, tail, prio, share, inj, cap_table, jam_table, coef = fixed
    head_row = lax.axis_index("corr") == 0
    plan_a, plan_b, plan_ra, plan_rb = routes

    def statics(read, base):
        cap = [pick(whole(read(base + i)), cap_table, 8) for i in range(LANES)]
        jam = [pick(whole(read(base + 4 + i)), jam_table, 4) for i in range(LANES)]
        wave = [wave_of(c, j) for c, j in zip(cap, jam)]
        return cap, jam, wave, [read(base + 8 + p) for p in range(LANES - 1)]

    head_fixed = [statics(head, HEAD_DEPTH * d + 16) for d in range(4)]
    tail_fixed = [statics(tail, TAIL_DEPTH * d + 24) for d in range(4)]

    def first(read, base):
        return [[read(base + i * CLASSES + k) for k in range(CLASSES)] for i in range(LANES)]

    def supplies(state, fixed):
        return [
            supply_of(total_of(state[i]), fixed[0][i], fixed[1][i], fixed[2][i])
            for i in range(LANES)
        ]

    def fluxes(state, fixed, next_supply):
        out = []
        for i in range(LANES):
            q = sent_share(total_of(state[i]), fixed[0][i], next_supply[i])
            out.append([x * q for x in state[i]])
        return out

    heads, tails = {}, {}
    for step in range(STEPS):
        if step < 4:
            heads[step] = first(head, HEAD_DEPTH * step)
            tails[step] = first(tail, TAIL_DEPTH * step)
        deep = min(step, 6 - step)
        supply = supplies(heads[0], head_fixed[0])
        arriving, rates = [], []
        for i in range(LANES):
            state = tails[0][i]
            speed = jnp.minimum(0.5, tail_fixed[0][0][i] * inverse(total_of(state)))
            demand = [x * speed for x in state]
            part_a = [share * x for x in demand]
            part_b = [x - y for x, y in zip(demand, part_a)]
            take_a = [permute(x, plan_a) for x in part_a]
            take_b = [permute(x, plan_b) for x in part_b]
            need_a = total_of(take_a)
            need_b = total_of(take_b)
            s = supply[i]
            share_a = prio * s
            share_b = (1.0 - prio) * s
            pass_a = jnp.minimum(need_a, middle(need_a, s - need_b, share_a))
            pass_b = jnp.minimum(need_b, middle(need_b, s - need_a, share_b))
            rate_a = pass_a / need_a
            rate_b = pass_b / need_b
            ramp = jnp.minimum(
                head(RAMP_ROW + step * LANES + i) * RAMP_UNIT,
                jnp.maximum((s - pass_a) - pass_b, 0.0),
            )
            arriving.append(
                [
                    (take_a[k] * rate_a + take_b[k] * rate_b) + RAMP_FRACTION[k] * ramp
                    for k in range(CLASSES)
                ]
            )
            back_a = permute(rate_a, plan_ra)
            back_b = permute(rate_b, plan_rb)
            rates.append([part_a[k] * back_a + part_b[k] * back_b for k in range(CLASSES)])
        for i in range(LANES):
            for k in range(CLASSES):
                inj[pl.ds((step * 12 + i * CLASSES + k) * 8, 8), :] = jnp.where(
                    head_row, arriving[i][k], rates[i][k]
                )
        if step == STEPS - 1:
            break
        new_heads, new_tails = {}, {}
        came, gone = arriving, rates
        for d in range(deep + 1):
            if d < deep or deep < step:
                ahead = supplies(heads[d + 1], head_fixed[d + 1])
                entering = fluxes(tails[d + 1], tail_fixed[d + 1], supplies(tails[d], tail_fixed[d]))
            else:
                ahead = [head(HEAD_DEPTH * d + 12 + i) for i in range(LANES)]
                entering = first(tail, TAIL_DEPTH * d + 12)
            out = fluxes(heads[d], head_fixed[d], ahead)
            moved = [
                [(heads[d][i][k] + came[i][k]) - out[i][k] for k in range(CLASSES)]
                for i in range(LANES)
            ]
            new_heads[d] = lane_change(moved, head_fixed[d][3], coef)
            moved = [
                [(tails[d][i][k] + entering[i][k]) - gone[i][k] for k in range(CLASSES)]
                for i in range(LANES)
            ]
            new_tails[d] = lane_change(moved, tail_fixed[d][3], coef)
            came, gone = out, entering
        heads, tails = new_heads, new_tails


def edge_kernel(
    cap_table, jam_table, coef_ref, strip, left, right,
    e0, e1, e2, e3, e4, e5, e6, e7, inner, rim, segment, aux, acc_out, low,
    nat, zone, inj, spare_rows, table, st, tot, cap, jam, wave, adj, level, acc,
):
    row = lax.axis_index("corr")
    place = lax.axis_index("lc")
    coef = [coef_ref[k] for k in range(CLASSES)]
    first_row = row == 0
    last_row = row == ROWS - 1

    @pl.when(jnp.logical_or(first_row, last_row))
    def _():
        for n, ends in enumerate((e0, e1, e2, e3, e4, e5, e6, e7)):
            chip = (place // 2 + (4 - n % 4)) % 4
            core = place % 2 if n < 4 else 1 - place % 2
            for m in range(2):
                side = jnp.where(first_row, m, 1 - m)
                base = side * (RECORD * 8) + 2 * chip + core
                for r in range(RECORD // 8):
                    zone[pl.ds(base + r * 64, 8, stride=8), :] = ends[
                        pl.ds(m * RECORD + r * 8, 8), :
                    ]
        junctions(zone, inj, spare_rows, table, cap_table, jam_table, coef)

    for i in range(23):
        nat[pl.ds(i * 48, 8), :] = left[pl.ds(i * 8, 8), :]
        nat[pl.ds(i * 48 + 8, 32), :] = strip[pl.ds(i * 32, 32), :]
        nat[pl.ds(i * 48 + 40, 8), :] = right[pl.ds(i * 8, 8), :]

    def rows_of(base):
        def read(i, rows):
            return nat[pl.ds((base + i) * 48 + rows.start, 8, stride=6), :]

        return read

    def code_of(base):
        read = rows_of(base)
        return lambda i, rows: read(i, rows).astype(jnp.int32)

    fill(
        6, 6, (st, tot, cap, jam, wave, adj, level, acc),
        rows_of(0), code_of(12), code_of(16), rows_of(20), cap_table, jam_table,
    )
    sub = lax.broadcasted_iota(jnp.int32, (8, WIDTH), 0)
    in_strip = sub % 4
    at_head = jnp.logical_and(sub == 1, first_row)
    at_tail = jnp.logical_and(sub == 6, last_row)

    def one(step, carry):
        def injected(i, k):
            return jnp.broadcast_to(
                inj[pl.ds((step * 12 + i * CLASSES + k) * 8 + place, 1), :], (8, WIDTH)
            )

        def inject(v, before, leaving):
            came, gone = before, leaving
            if v == 2:
                came = [
                    [jnp.where(at_head, injected(i, k), before[i][k]) for k in range(CLASSES)]
                    for i in range(LANES)
                ]
            if v == 3:
                gone = [
                    [jnp.where(at_tail, injected(i, k), leaving[i][k]) for k in range(CLASSES)]
                    for i in range(LANES)
                ]
            return came, gone

        def mask(v):
            if v < 2:
                return in_strip == 2
            if v < 4:
                return jnp.logical_or(in_strip == 1, in_strip == 2)
            return in_strip == 1

        def scan(running, lowest):
            second = in_strip == 2
            carry = jnp.where(second, pltpu.roll(running, 1, 0), 0.0)
            floor = jnp.where(second, pltpu.roll(lowest, 1, 0), BIG)
            total = carry + running
            least = jnp.minimum(floor, carry + lowest)
            aux[0, pl.ds(step, 1), :] = total[2:3, :]
            aux[1, pl.ds(step, 1), :] = least[2:3, :]
            aux[2, pl.ds(step, 1), :] = total[6:7, :]
            aux[3, pl.ds(step, 1), :] = least[6:7, :]
            return carry, floor

        window(
            6, (st, tot, cap, jam, wave, adj, level, acc, low), step, coef, inject, mask, scan
        )
        return carry

    lax.fori_loop(0, STEPS, one, 0)
    for v in range(6):
        for i in range(LANES * CLASSES):
            nat[pl.ds(i * 48 + v, 8, stride=6), :] = st[i, v]
        acc_out[v] = acc[0, v]
    for i in range(LANES * CLASSES):
        rim[0, i] = nat[pl.ds(i * 48 + 8, 8), :]
        rim[1, i] = nat[pl.ds(i * 48 + 32, 8), :]
    left_sum, left_low = aux[0], aux[1]
    most_sum = left_sum + inner[0]
    most_low = jnp.minimum(left_low, left_sum + inner[1])
    all_sum = most_sum + aux[2]
    all_low = jnp.minimum(most_low, most_sum + aux[3])
    for i in range(ROWS):
        segment[i, 0] = all_sum
        segment[i, 1] = all_low


def count_kernel(
    segments, aux, inner, acc, early_low, late_low, edge_acc, edge_low, rim, traffic_in,
    queue, traffic, sums, floors, nat, sem,
):
    del traffic_in
    copies = [
        pltpu.make_async_copy(rim.at[0], traffic.at[:, pl.ds(0, 8), :], sem.at[0]),
        pltpu.make_async_copy(rim.at[1], traffic.at[:, pl.ds(CELLS_HERE - 8, 8), :], sem.at[1]),
    ]
    for copy in copies:
        copy.start()
    row = lax.axis_index("corr")
    total = jnp.zeros((8, WIDTH), F32)
    least = jnp.zeros((8, WIDTH), F32)
    for i in range(ROWS - 1):
        on = i < row
        least = jnp.where(on, jnp.minimum(least, total + segments[i, 1]), least)
        total = jnp.where(on, total + segments[i, 0], total)
    mid_total = total + aux[0]
    mid_least = jnp.minimum(least, total + aux[1])
    end_total = mid_total + inner[0]
    end_least = jnp.minimum(mid_least, mid_total + inner[1])
    for n, (t, m) in enumerate(((total, least), (mid_total, mid_least), (end_total, end_least))):
        sums[n] = t
        floors[n] = m
    scale = 1.0 / (STEPS * CELLS_HERE * ROWS)
    left = lax.broadcasted_iota(jnp.int32, (8, WIDTH), 0) < 4

    def spread(ref, n, step):
        return jnp.broadcast_to(ref[n, pl.ds(step, 1), :], (8, WIDTH))

    inside = [(spread(sums, 1, s), spread(floors, 1, s)) for s in range(STEPS)]
    for v in range(16):
        value = acc[v]
        for s in range(STEPS):
            value = value + (inside[s][0] - jnp.minimum(inside[s][1], inside[s][0] + (early_low if s < HALF else late_low)[s, v]))
        queue[pl.ds(v, 8, stride=16), :] = value * scale
    edges = [
        (
            jnp.where(left, spread(sums, 0, s), spread(sums, 2, s)),
            jnp.where(left, spread(floors, 0, s), spread(floors, 2, s)),
        )
        for s in range(STEPS)
    ]
    for v in range(6):
        value = edge_acc[v]
        for s in range(STEPS):
            value = value + (edges[s][0] - jnp.minimum(edges[s][1], edges[s][0] + edge_low[s, v]))
        nat[pl.ds(v, 8, stride=6), :] = value * scale
    queue[pl.ds(0, 8), :] = nat[pl.ds(8, 8), :]
    queue[pl.ds(CELLS_HERE - 8, 8), :] = nat[pl.ds(32, 8), :]
    for copy in copies:
        copy.wait()


def shape(*dims):
    return jax.ShapeDtypeStruct(dims, F32)


def full(*dims):
    return pl.BlockSpec(dims, lambda i: (0,) * len(dims))


def part(place, *dims):
    return pl.BlockSpec(dims, lambda i: (0, place, 0))


SCALARS = pl.BlockSpec(memory_space=pltpu.SMEM)
HERE = pl.BlockSpec(memory_space=pltpu.VMEM)


def call(kernel, name, args, in_specs, outs, out_specs, scratch=(), aliases=None, flops=0, vmem=32, grid=(1,)):
    return pl.pallas_call(
        kernel,
        grid=grid,
        in_specs=in_specs,
        out_specs=out_specs,
        out_shape=outs,
        scratch_shapes=scratch,
        input_output_aliases=aliases or {},
        compiler_params=pltpu.CompilerParams(vmem_limit_bytes=vmem << 20),
        cost_estimate=pl.CostEstimate(flops=flops, bytes_accessed=4 << 20, transcendentals=0),
        name=name,
    )(*args)


def cells_scratch(count):
    def hold(n):
        return pltpu.VMEM((n, count, 8, WIDTH), F32)

    return [hold(12), hold(4), hold(4), hold(4), hold(4), hold(3), pltpu.VMEM((count, 8, WIDTH), F32), hold(2)]


def on_device(
    density, cap_code, jam_code, adjacency, ramp_code, feed_a, feed_b, turn_share, priority,
    cap_table, jam_table, change_coef,
):
    density = density.reshape(12, CELLS_HERE, WIDTH)
    tables = [cap_table, jam_table, change_coef]
    grids = [density, cap_code, jam_code, adjacency]
    sizes = (12, 4, 4, 3)

    def ends(depth):
        args, specs = [], []
        for x, n in zip(grids, sizes):
            args += [x, x]
            specs += [part(0, n, depth, WIDTH), part(CELLS_HERE // depth - 1, n, depth, WIDTH)]
        return args, specs

    args, specs = ends(8)
    line = [x.reshape(1, WIDTH) for x in (feed_a, feed_b, turn_share, priority)]
    fwd, bwd, both = call(
        pack_kernel, "pack",
        tables + [feed_a, feed_b] + line + [ramp_code.reshape(32, WIDTH)] + args,
        [SCALARS] * 5 + [full(1, WIDTH)] * 4 + [full(32, WIDTH)] + specs,
        [shape(184, WIDTH), shape(184, WIDTH), shape(2 * RECORD, WIDTH)],
        [full(184, WIDTH), full(184, WIDTH), full(2 * RECORD, WIDTH)],
        vmem=60,
    )
    left = lax.ppermute(fwd, "corr", [(i, (i + 1) % ROWS) for i in range(ROWS)])
    right = lax.ppermute(bwd, "corr", [((i + 1) % ROWS, i) for i in range(ROWS)])
    def cells(n):
        return (n, 16, 8, WIDTH)

    held = [cells(12), cells(4), cells(4), cells(4), cells(4), cells(3), (16, 8, WIDTH), cells(2)]
    early_low, inner, strip, *state = call(
        early_kernel, "early", tables + grids,
        [SCALARS] * 3 + [full(n, CELLS_HERE, WIDTH) for n in sizes],
        [shape(8, 16, 8, WIDTH), shape(2, 8, WIDTH), shape(23 * 32, WIDTH)]
        + [shape(*x) for x in held],
        [full(8, 16, 8, WIDTH), full(2, 8, WIDTH), full(23 * 32, WIDTH)]
        + [full(*x) for x in held],
        flops=1 << 26,
    )
    left, right, inner = lax.optimization_barrier((left, right, inner))
    other_end = jnp.where(lax.axis_index("corr") == 0, left[:RECORD], right[:RECORD])
    both = lax.dynamic_update_slice(both, other_end, (RECORD, 0))
    both, state = lax.optimization_barrier((both, tuple(state)))
    pieces = [both] + [
        lax.ppermute(both, "lc", [(i, (i + 2 * k) % 8) for i in range(8)]) for k in (1, 2, 3)
    ]
    traffic, acc, late_low, inner = call(
        late_kernel, "late", [change_coef, inner] + list(state),
        [SCALARS, full(2, 8, WIDTH)] + [full(*x) for x in held],
        [shape(12, CELLS_HERE, WIDTH), shape(16, 8, WIDTH), shape(8, 16, 8, WIDTH), shape(2, 8, WIDTH)],
        [full(12, CELLS_HERE, WIDTH), full(16, 8, WIDTH), full(8, 16, 8, WIDTH), full(2, 8, WIDTH)],
        [pltpu.VMEM(cells(12), F32), pltpu.VMEM(cells(4), F32), pltpu.VMEM(cells(2), F32)],
        flops=1 << 26,
    )
    swap = [(i, i ^ 1) for i in range(8)]
    swapped = [lax.ppermute(both, "lc", swap)]
    for n in (1, 2, 3):
        pieces[n], inner = lax.optimization_barrier((pieces[n], inner))
        swapped.append(lax.ppermute(pieces[n], "lc", swap))
    pieces = pieces + swapped
    any_space = pl.BlockSpec(memory_space=pl.ANY)
    rim, segment, aux, edge_acc, edge_low = call(
        edge_kernel, "edges",
        tables + [strip, left, right] + pieces + [inner],
        [SCALARS] * 3 + [HERE] * 12,
        [shape(2, 12, 8, WIDTH), shape(ROWS, 2, 8, WIDTH), shape(4, 8, WIDTH),
         shape(6, 8, WIDTH), shape(8, 6, 8, WIDTH)],
        [HERE] * 5,
        [pltpu.VMEM((23 * 48, WIDTH), F32), pltpu.VMEM((2 * RECORD * 8, WIDTH), F32),
         pltpu.VMEM((STEPS * 12 * 8, WIDTH), F32), pltpu.VMEM((16, WIDTH), F32),
         pltpu.VMEM((64, WIDTH), jnp.int32)]
        + cells_scratch(6),
        grid=(),
    )
    segments = lax.all_to_all(segment, "corr", 0, 0)
    queue, traffic = call(
        count_kernel, "count",
        [segments, aux, inner, acc, early_low, late_low, edge_acc, edge_low, rim, traffic],
        [HERE] * 9 + [any_space],
        [shape(CELLS_HERE, WIDTH), shape(12, CELLS_HERE, WIDTH)], [HERE, any_space],
        [pltpu.VMEM((3, 8, WIDTH), F32), pltpu.VMEM((3, 8, WIDTH), F32), pltpu.VMEM((48, WIDTH), F32),
         pltpu.SemaphoreType.DMA((2,))],
        aliases={9: 1}, grid=(),
    )
    return traffic.reshape(LANES, CLASSES, CELLS_HERE, WIDTH), queue


def solution(mesh):
    placed = (
        P(None, None, "corr", "lc"),
        P(None, "corr", "lc"),
        P(None, "corr", "lc"),
        P(None, "corr", "lc"),
        P(None, None, "lc"),
        P("lc"),
        P("lc"),
        P("lc"),
        P("lc"),
        P(),
        P(),
        P(),
    )
    return jax.shard_map(
        on_device,
        mesh=mesh,
        in_specs=placed,
        out_specs=(P(None, None, "corr", "lc"), P("corr", "lc")),
        check_vma=False,
    )
```
